256 devices in a mesh: graph: 32 (over y, x, core), rep: 8 (over z).
Axes of the slice: x: 4, y: 4, z: 8, core: 2. Of those that a mesh axis runs over, the one named last changes fastest.
Arguments:
- nodes: bfloat16 [8, 1024, 32, 256], P('rep', 'graph'), may hold values from -20 to 20, as said below
- cotangent: bfloat16 [8, 1024, 32, 256], P('rep', 'graph'), may hold values from -6 to 6
- live: int32 [8, 1024], P('rep', 'graph'), may hold values from 2 to 32, as said below
- partner_first: int32 [8, 1024], P('rep', 'graph'), may hold values from 0 to 1023, as said below
- partner_size: int32 [8, 1024], P('rep', 'graph'), may hold values from 1 to 2
- edge_src: int32 [8, 32768], P('rep', 'graph'), may hold values from 0 to 1023, as said below
- edge_dst: int32 [8, 32768], P('rep', 'graph'), may hold values from 0 to 1023, as said below
- w_edge1: bfloat16 [512, 512], replicated, may hold values from -0.25 to 0.25
- b_edge: float32 [512], replicated, may hold values from -3 to 3
- w_edge2: bfloat16 [512, 256], replicated, may hold values from -0.25 to 0.25
- w_node1: bfloat16 [768, 512], replicated, may hold values from -0.21875 to 0.21875
- b_node: float32 [512], replicated, may hold values from -3 to 3
- w_node2: bfloat16 [512, 256], replicated, may hold values from -0.25 to 0.25
Outputs:
- updated: bfloat16 [8, 1024, 32, 256], P('rep', 'graph')
- d_nodes: bfloat16 [8, 1024, 32, 256], P('rep', 'graph')
- g_edge1: float32 [512, 512], P('rep')
- g_bedge: float32 [512], P('rep')
- g_edge2: float32 [512, 256], P('rep')
- g_node1: float32 [768, 512], P('rep')
- g_bnode: float32 [512], P('rep')
- g_node2: float32 [512, 256], P('rep')
The draws below stay inside these ranges and needn't reach their ends.
Inputs may be any that keep to these rules, and one draw needn't show every extreme that they name: A graph is one or two consecutive granules of one device, and every granule of a graph but its last is full; rows beyond live are padding. `partner_first`: index within the replica of the first granule of the partner graph, the same for all granules of a graph; pairing is mutual. Graphs in the lower half of a device's 32 granules pair with graphs in the upper half of some device's granules; the upper-half graphs of one device have partners on distinct devices. Within a replica every half of every device holds the same number of two-granule graphs. `edge_src`: row index within the device (granule times 32 plus row); both ends of an edge are live rows of the same graph. `edge_dst`: as edge_src. `nodes`: padding rows are zero.
All inputs are finite; a program needn't handle non-finite values.
Results may differ from the reference program's by a relative error of at most 0.023.
Values may be sent and summed in bfloat16 or wider, within the bound.
No kernel may reach another device: no remote copies, remote signals or barrier semaphores. Data moves between devices by JAX's collectives and lax.ppermute only.
A program may use at most 128 MiB of HBM per device.

```python
import jax
import jax.numpy as jnp
from jax import lax

H = 256
FM = 512
BLK = 32
GMAX = 2
NB = 32
E_DEV = 1024
G_ALL = 1024
N_GRAPH = 32
N_REP = 8


def inverse_order(ordering):
    return jnp.zeros(ordering.shape, jnp.int32).at[ordering].set(jnp.arange(ordering.shape[0], dtype=jnp.int32))


def device_orders(stream):
    streams = jax.random.split(stream, N_GRAPH)
    return jax.vmap(lambda single: inverse_order(jax.random.permutation(single, N_GRAPH).astype(jnp.int32)))(streams)


def pick(member, lookup):
    return jnp.sum(jnp.where(member, lookup, 0), axis=2).astype(jnp.int32)


def layout_one(replica_key):
    peer_count = N_GRAPH
    half_count = NB // 2
    streams = jax.random.split(jax.random.fold_in(replica_key, 17), 8)
    lowest = max(half_count - peer_count, 1)
    highest = half_count // 2
    double_count = jax.random.randint(streams[0], (), lowest, highest + 1)
    graph_count = half_count - double_count
    offsets = jnp.arange(peer_count, dtype=jnp.int32)
    first_order = inverse_order(jax.random.permutation(streams[1], peer_count).astype(jnp.int32))
    active = first_order < graph_count
    size_moving = jnp.where(active, jnp.where(first_order < double_count, 2, 1), 0).astype(jnp.int32)
    second_order = inverse_order(jax.random.permutation(streams[2], peer_count).astype(jnp.int32))
    rank_active = jnp.sum(active[None, :] & (second_order[None, :] < second_order[:, None]), axis=1)
    size_staying = jnp.where(active, jnp.where(rank_active < double_count, 2, 1), 0).astype(jnp.int32)
    sigma = jax.random.permutation(streams[3], peer_count).astype(jnp.int32)
    sigma_inverse = inverse_order(sigma)
    tau = jax.random.permutation(streams[4], peer_count).astype(jnp.int32)
    tau_inverse = inverse_order(tau)
    order_moving = device_orders(streams[5])
    order_staying = device_orders(streams[6])
    start_moving = jnp.sum(size_moving[None, None, :] * (order_moving[:, None, :] < order_moving[:, :, None]), axis=2).astype(jnp.int32)
    start_staying = jnp.sum(size_staying[None, None, :] * (order_staying[:, None, :] < order_staying[:, :, None]), axis=2).astype(jnp.int32)
    staying_device = sigma_inverse[(tau[:, None] + offsets[None, :]) % peer_count]
    moving_device = tau_inverse[(sigma[:, None] - offsets[None, :]) % peer_count]
    spots = jnp.arange(half_count, dtype=jnp.int32)
    member_staying = active[None, None, :] & (start_staying[:, None, :] <= spots[None, :, None]) & (spots[None, :, None] < start_staying[:, None, :] + size_staying[None, None, :])
    member_moving = active[None, None, :] & (start_moving[:, None, :] <= spots[None, :, None]) & (spots[None, :, None] < start_moving[:, None, :] + size_moving[None, None, :])
    offset_low = pick(member_staying, offsets[None, None, :])
    first_low = pick(member_staying, start_staying[:, None, :])
    size_low = pick(member_staying, size_staying[None, None, :])
    mate_low = jnp.take_along_axis(moving_device, offset_low, axis=1)
    partner_low = mate_low * NB + half_count + start_moving[mate_low, offset_low]
    mate_size_low = size_moving[offset_low]
    offset_high = pick(member_moving, offsets[None, None, :])
    first_high = pick(member_moving, start_moving[:, None, :]) + half_count
    size_high = pick(member_moving, size_moving[None, None, :])
    mate_high = jnp.take_along_axis(staying_device, offset_high, axis=1)
    partner_high = mate_high * NB + start_staying[mate_high, offset_high]
    mate_size_high = size_staying[offset_high]
    partner = jnp.concatenate([partner_low, partner_high], axis=1).astype(jnp.int32)
    partner_sizes = jnp.concatenate([mate_size_low, mate_size_high], axis=1).astype(jnp.int32)
    own_local = jnp.concatenate([first_low, first_high], axis=1)
    own_size = jnp.concatenate([size_low, size_high], axis=1)
    place_index = jnp.arange(NB, dtype=jnp.int32)[None, :] - own_local
    lowest_live = max(2, BLK // 4)
    live_counts = jax.random.randint(streams[7], (peer_count, NB), lowest_live, BLK + 1)
    live_counts = jnp.where((own_size == 2) & (place_index == 0), BLK, live_counts).astype(jnp.int32)
    own_first = (jnp.arange(peer_count, dtype=jnp.int32)[:, None] * NB + own_local).astype(jnp.int32)
    return (live_counts.reshape(-1), partner.reshape(-1), partner_sizes.reshape(-1), own_first.reshape(-1), own_size.reshape(-1).astype(jnp.int32))


def edges_one(replica_key):
    live_counts, partner, partner_sizes, own_first, own_size = layout_one(replica_key)
    streams = jax.random.split(jax.random.fold_in(replica_key, 29), 4)
    device_base = jnp.arange(N_GRAPH, dtype=jnp.int32)[:, None] * NB
    target_local = jax.random.randint(streams[0], (N_GRAPH, E_DEV), 0, NB)
    target_granule = device_base + target_local
    target_row = jax.random.randint(streams[1], (N_GRAPH, E_DEV), 0, live_counts[target_granule])
    source_granule = own_first[target_granule] + jax.random.randint(streams[2], (N_GRAPH, E_DEV), 0, own_size[target_granule])
    source_row = jax.random.randint(streams[3], (N_GRAPH, E_DEV), 0, live_counts[source_granule])
    source_local = (source_granule - device_base) * BLK + source_row
    target_flat = target_local * BLK + target_row
    return (source_local.reshape(-1).astype(jnp.int32), target_flat.reshape(-1).astype(jnp.int32))


def nodes_one(replica_key):
    live_counts, partner, partner_sizes, own_first, own_size = layout_one(replica_key)
    streams = jax.random.split(jax.random.fold_in(replica_key, 41), 1)
    granules = N_GRAPH * NB
    values = jnp.clip(jax.random.normal(streams[0], (granules, BLK, H), jnp.float32), -6.0, 6.0)
    row_live = jnp.arange(BLK, dtype=jnp.int32)[None, :] < live_counts[:, None]
    return jnp.where(row_live[:, :, None], values, 0.0)


def over_replicas(key, maker):
    return jax.vmap(lambda replica_index: maker(jax.random.fold_in(key, replica_index)))(jnp.arange(N_REP, dtype=jnp.int32))


def draw_nodes(key, part):
    return over_replicas(key, nodes_one).astype(jnp.bfloat16)


def draw_live(key, part):
    return over_replicas(key, lambda replica_key: layout_one(replica_key)[0])


def draw_partner_first(key, part):
    return over_replicas(key, lambda replica_key: layout_one(replica_key)[1])


def draw_partner_size(key, part):
    return over_replicas(key, lambda replica_key: layout_one(replica_key)[2])


def draw_edge_src(key, part):
    return over_replicas(key, lambda replica_key: edges_one(replica_key)[0])


def draw_edge_dst(key, part):
    return over_replicas(key, lambda replica_key: edges_one(replica_key)[1])


def level_of(rng, extent, cuts, smallest, high):
    def one(dim, blocks):
        draws = jax.random.uniform(jax.random.fold_in(jax.random.fold_in(rng, 6), dim), (blocks,), jnp.float32, smallest / len(cuts), high / len(cuts))
        return jnp.repeat(jnp.exp(draws), extent[dim] // blocks).reshape((-1,) + (1,) * (len(extent) - dim - 1))

    level = one(*cuts[0])
    for cut in cuts[1:]:
        level = level * one(*cut)
    return level


def centred(key, extent, deviation, bound, cuts=(), kind=jnp.bfloat16):
    result = jax.random.normal(key, extent, jnp.float32) * deviation
    if len(cuts) > 0:
        result = level_of(key, extent, cuts, -0.22, 0.18) * result
    return jnp.clip(result, min=-bound, max=bound).astype(kind)


def setup_inputs(seed: int = 0) -> dict:
    key_of = jax.random.split(jax.random.key(seed), 14)
    return {
        "nodes": draw_nodes(jax.random.fold_in(key_of[13], 71), 0),
        "cotangent": centred(key_of[1], (N_REP, G_ALL, BLK, H), 1.0, 6.0, ((0, 8), (1, 32))),
        "live": draw_live(jax.random.fold_in(key_of[13], 71), 0),
        "partner_first": draw_partner_first(jax.random.fold_in(key_of[13], 71), 0),
        "partner_size": draw_partner_size(jax.random.fold_in(key_of[13], 71), 0),
        "edge_src": draw_edge_src(jax.random.fold_in(key_of[13], 71), 0),
        "edge_dst": draw_edge_dst(jax.random.fold_in(key_of[13], 71), 0),
        "w_edge1": centred(key_of[7], (2 * H, FM), (2 * H) ** -0.5, 0.25),
        "b_edge": centred(key_of[8], (FM,), 0.5, 3.0, (), jnp.float32),
        "w_edge2": centred(key_of[9], (FM, H), FM ** -0.5, 0.25),
        "w_node1": centred(key_of[10], (3 * H, FM), (3 * H) ** -0.5, 0.21875),
        "b_node": centred(key_of[11], (FM,), 0.5, 3.0, (), jnp.float32),
        "w_node2": centred(key_of[12], (FM, H), FM ** -0.5, 0.25),
    }


def silu_slope(values):
    sigmoid_value = jax.nn.sigmoid(values)
    return sigmoid_value * (1.0 + values * (1.0 - sigmoid_value))


def attend(queries, key_rows, key_mask):
    scale_factor = queries.shape[-1] ** -0.5
    scores = jnp.einsum("gqh,gkh->gqk", queries.astype(jnp.float32), key_rows.astype(jnp.float32), precision=lax.Precision.HIGHEST) * scale_factor
    scores = jnp.where(key_mask[:, None, :], scores, -jnp.inf)
    highest = jnp.max(scores, axis=-1, keepdims=True)
    powers = jnp.exp(scores - highest)
    softmax_out = powers / jnp.sum(powers, axis=-1, keepdims=True)
    softmax_low = softmax_out.astype(jnp.bfloat16)
    context = jnp.einsum("gqk,gkh->gqh", softmax_low.astype(jnp.float32), key_rows.astype(jnp.float32), precision=lax.Precision.HIGHEST)
    moved_rows = (queries.astype(jnp.float32) - context).astype(jnp.bfloat16)
    return moved_rows, softmax_out, softmax_low


def attend_back(queries, key_rows, softmax_out, softmax_low, grad_moved):
    scale_factor = queries.shape[-1] ** -0.5
    negated = (-grad_moved).astype(jnp.float32)
    keys_wide = key_rows.astype(jnp.float32)
    grad_probs = jnp.einsum("gqh,gkh->gqk", negated, keys_wide, precision=lax.Precision.HIGHEST)
    grad_keys = jnp.einsum("gqk,gqh->gkh", softmax_low.astype(jnp.float32), negated, precision=lax.Precision.HIGHEST)
    inner_sum = jnp.sum(softmax_out * grad_probs, axis=-1, keepdims=True)
    grad_scores = (softmax_out * (grad_probs - inner_sum) * scale_factor).astype(jnp.bfloat16)
    scores_wide = grad_scores.astype(jnp.float32)
    grad_queries = jnp.einsum("gqk,gkh->gqh", scores_wide, keys_wide, precision=lax.Precision.HIGHEST) + grad_moved.astype(jnp.float32)
    grad_keys = grad_keys + jnp.einsum("gqk,gqh->gkh", scores_wide, queries.astype(jnp.float32), precision=lax.Precision.HIGHEST)
    return grad_queries, grad_keys


def replica(nodes, cotangent, live, partner_first, partner_size, edge_src, edge_dst, w_edge1, b_edge, w_edge2, w_node1, b_node, w_node2):
    granules, block_rows, state_width = nodes.shape
    node_rows = nodes.reshape(-1, state_width)
    total_rows = node_rows.shape[0]
    positions = jnp.arange(block_rows, dtype=jnp.int32)
    row_mask = (positions[None, :] < live[:, None]).reshape(-1, 1)
    offsets = (jnp.arange(edge_src.shape[0], dtype=jnp.int32) // E_DEV) * (NB * block_rows)
    sources = (edge_src + offsets).astype(jnp.int32)
    targets = (edge_dst + offsets).astype(jnp.int32)

    pre_target = (jnp.dot(node_rows, w_edge1[:state_width], preferred_element_type=jnp.float32) + b_edge).astype(jnp.bfloat16)
    pre_source = jnp.dot(node_rows, w_edge1[state_width:], preferred_element_type=jnp.float32).astype(jnp.bfloat16)
    summed = pre_target[targets].astype(jnp.float32) + pre_source[sources].astype(jnp.float32)
    gathered = jax.ops.segment_sum(jax.nn.silu(summed), targets, num_segments=total_rows).astype(jnp.bfloat16)
    message = jnp.dot(gathered, w_edge2, preferred_element_type=jnp.float32).astype(jnp.bfloat16)

    key_index = jnp.minimum(partner_first[:, None] + jnp.arange(GMAX, dtype=jnp.int32)[None, :], granules - 1).astype(jnp.int32)
    size_mask = jnp.arange(GMAX, dtype=jnp.int32)[None, :] < partner_size[:, None]
    key_mask = (size_mask[:, :, None] & (positions[None, None, :] < live[key_index][:, :, None])).reshape(granules, GMAX * block_rows)
    key_rows = nodes[key_index].reshape(granules, GMAX * block_rows, state_width)
    moved_rows, softmax_out, softmax_low = attend(nodes, key_rows, key_mask)
    moved_flat = moved_rows.reshape(-1, state_width)

    hidden_pre = (jnp.dot(node_rows, w_node1[:state_width], preferred_element_type=jnp.float32)
                  + jnp.dot(message, w_node1[state_width:2 * state_width], preferred_element_type=jnp.float32)
                  + jnp.dot(moved_flat, w_node1[2 * state_width:], preferred_element_type=jnp.float32) + b_node)
    active = jax.nn.silu(hidden_pre).astype(jnp.bfloat16)
    updated = jnp.where(row_mask, node_rows.astype(jnp.float32) + jnp.dot(active, w_node2, preferred_element_type=jnp.float32), 0.0).astype(jnp.bfloat16)

    grad_out = jnp.where(row_mask, cotangent.reshape(-1, state_width), jnp.zeros((), jnp.bfloat16)).astype(jnp.bfloat16)
    g_node2 = jnp.dot(active.T, grad_out, preferred_element_type=jnp.float32)
    grad_hidden = (jnp.dot(grad_out, w_node2.T, preferred_element_type=jnp.float32) * silu_slope(hidden_pre)).astype(jnp.bfloat16)
    g_node1 = jnp.concatenate([jnp.dot(node_rows.T, grad_hidden, preferred_element_type=jnp.float32),
                               jnp.dot(message.T, grad_hidden, preferred_element_type=jnp.float32),
                               jnp.dot(moved_flat.T, grad_hidden, preferred_element_type=jnp.float32)], axis=0)
    g_bnode = jnp.sum(grad_hidden.astype(jnp.float32), axis=0)
    grad_rows = grad_out.astype(jnp.float32) + jnp.dot(grad_hidden, w_node1[:state_width].T, preferred_element_type=jnp.float32)
    grad_message = jnp.dot(grad_hidden, w_node1[state_width:2 * state_width].T, preferred_element_type=jnp.float32).astype(jnp.bfloat16)
    grad_moved = jnp.dot(grad_hidden, w_node1[2 * state_width:].T, preferred_element_type=jnp.float32).astype(jnp.bfloat16)

    grad_queries, grad_keys = attend_back(nodes, key_rows, softmax_out, softmax_low, grad_moved.reshape(granules, block_rows, state_width))
    attention_grad = grad_queries.at[key_index.reshape(-1)].add(grad_keys.reshape(granules * GMAX, block_rows, state_width))

    g_edge2 = jnp.dot(gathered.T, grad_message, preferred_element_type=jnp.float32)
    grad_gathered = jnp.dot(grad_message, w_edge2.T, preferred_element_type=jnp.float32).astype(jnp.bfloat16)
    edge_grad = grad_gathered[targets].astype(jnp.float32) * silu_slope(summed)
    grad_target = jax.ops.segment_sum(edge_grad, targets, num_segments=total_rows).astype(jnp.bfloat16)
    grad_source = jax.ops.segment_sum(edge_grad, sources, num_segments=total_rows).astype(jnp.bfloat16)
    g_edge1 = jnp.concatenate([jnp.dot(node_rows.T, grad_target, preferred_element_type=jnp.float32),
                               jnp.dot(node_rows.T, grad_source, preferred_element_type=jnp.float32)], axis=0)
    g_bedge = jnp.sum(grad_target.astype(jnp.float32), axis=0)
    grad_rows = (grad_rows + attention_grad.reshape(-1, state_width)
                 + jnp.dot(grad_target, w_edge1[:state_width].T, preferred_element_type=jnp.float32)
                 + jnp.dot(grad_source, w_edge1[state_width:].T, preferred_element_type=jnp.float32))
    d_nodes = jnp.where(row_mask, grad_rows, 0.0).astype(jnp.bfloat16)
    return (updated.reshape(granules, block_rows, state_width), d_nodes.reshape(granules, block_rows, state_width),
            g_edge1, g_bedge, g_edge2, g_node1, g_bnode, g_node2)


def reference(nodes, cotangent, live, partner_first, partner_size, edge_src, edge_dst, w_edge1, b_edge, w_edge2, w_node1, b_node, w_node2):
    def one_replica(inputs):
        return replica(inputs[0], inputs[1], inputs[2], inputs[3], inputs[4], inputs[5], inputs[6],
                       w_edge1, b_edge, w_edge2, w_node1, b_node, w_node2)

    results = lax.map(one_replica, (nodes, cotangent, live, partner_first, partner_size, edge_src, edge_dst))
    scale_factor = (N_REP * N_GRAPH * NB * BLK) ** -0.5
    grads = tuple(jnp.sum(item, axis=0) * scale_factor for item in results[2:])
    return (results[0], results[1], grads[0], grads[1], grads[2], grads[3], grads[4], grads[5])
```

```python
import functools

import jax
import jax.numpy as jnp
from jax import lax
from jax.experimental import pallas as pl
from jax.experimental.pallas import tpu as pltpu
from jax.sharding import PartitionSpec as P

F32 = jnp.float32
BF16 = jnp.bfloat16
GMAX = 2
LANES = 128
MARK = 16384.0
MARK_LIMIT = 8192.0
VMEM_LIMIT = 48 * 1024 * 1024


def mm(a, b):
    return jnp.dot(a, b, preferred_element_type=F32)


def mm_nt(a, b):
    return lax.dot_general(a, b, (((1,), (1,)), ((), ())), preferred_element_type=F32)


def mm_tn(a, b):
    return lax.dot_general(a, b, (((0,), (0,)), ((), ())), preferred_element_type=F32)


def sigmoid(v):
    return 1.0 / (1.0 + jnp.exp(-v))


def iota(shape, dim):
    return lax.broadcasted_iota(jnp.int32, shape, dim)


def live_rows(live_ref, first, count, block, width):
    limits = [jnp.full((block, width), live_ref[0, first + k], jnp.int32) for k in range(count)]
    positions = iota((block, width), 0)
    return jnp.concatenate([positions] * count, axis=0) < jnp.concatenate(limits, axis=0)


def one_hot(hit):
    return jnp.where(hit, 1.0, 0.0).astype(BF16)


def spread(row_ref):
    return jnp.transpose(jnp.broadcast_to(row_ref[...], (LANES, row_ref.shape[1])))


def by_edge(columns, rows):
    lanes = iota(columns.shape, 1)
    return jnp.concatenate(
        [one_hot(columns == lanes + k * LANES) for k in range(rows // LANES)], axis=1
    )


def by_row(row_ref, start, count):
    edges = row_ref.shape[1]
    return one_hot(
        jnp.broadcast_to(row_ref[...], (count, edges)) == iota((count, edges), 0) + start
    )


def pack_kernel(live_ref, first_ref, nodes_ref, out_ref):
    granules, block, width = nodes_ref.shape
    rows, columns = iota((block, width), 0), iota((block, width), 1)
    for g in range(granules):
        slot = (first_ref[0, g] // granules) * (2 * GMAX) + (GMAX if g < granules // 2 else 0)
        if g > 0:
            slot = slot + (first_ref[0, g] == first_ref[0, g - 1]).astype(jnp.int32)
        marked = (rows >= live_ref[0, g]) & (columns == 0)
        out_ref[slot] = jnp.where(marked, MARK, nodes_ref[g].astype(F32)).astype(BF16)


def edge_forward_kernel(
    src_ref, dst_ref, nodes_ref, w1_ref, b_ref, w2_ref,
    message_ref, gathered_ref, slope_ref,
    pre_t, pre_s, terms, col_t, col_s,
):
    rows, width = nodes_ref.shape
    edges = src_ref.shape[1]
    chunk = 256
    col_t[...] = spread(dst_ref)
    col_s[...] = spread(src_ref)
    for k in range(rows // chunk):
        at = pl.ds(k * chunk, chunk)
        x = nodes_ref[at, :]
        pre_t[at, :] = (mm(x, w1_ref[:width, :]) + b_ref[...]).astype(BF16)
        pre_s[at, :] = mm(x, w1_ref[width:, :]).astype(BF16)
    for k in range(edges // chunk):
        at = pl.ds(k * chunk, chunk)
        summed = mm(by_edge(col_t[at, :], rows), pre_t[...]) + mm(
            by_edge(col_s[at, :], rows), pre_s[...]
        )
        s = sigmoid(summed)
        terms[at, :] = (summed * s).astype(BF16)
        slope_ref[at, :] = (s * (1.0 + summed * (1.0 - s))).astype(BF16)
    for k in range(rows // chunk):
        at = pl.ds(k * chunk, chunk)
        gathered = mm(by_row(dst_ref, k * chunk, chunk), terms[...]).astype(BF16)
        gathered_ref[at, :] = gathered
        message_ref[at, :] = mm(gathered, w2_ref[...]).astype(BF16)


def deal(stage, value, first_row, per_rep, base, places, offset):
    rows, width = value.shape
    across = width // LANES
    for i in range(rows // 8):
        rep, inner = divmod(first_row + 8 * i, per_rep)
        for c in range(across):
            unit = base + (inner // 8) * across + c
            share, q = unit % 32, unit // 32
            at = (rep * places + q) * 8 + offset
            stage[share, pl.ds(at, 8), :] = value[8 * i : 8 * i + 8, c * LANES : (c + 1) * LANES]


def node_kernel(
    live_ref, first_ref, size_ref, nodes_ref, arrived_ref, cot_ref, message_ref, gathered_ref,
    w1_ref, b_ref, w2_ref,
    updated_ref, probs_ref, keys_ref, gmsg_ref, gmov_ref, base_ref, bias_ref, send_ref,
    scores, moved, active, hidden_grad, out_grad, stage,
):
    rows, width = nodes_ref.shape
    granules = live_ref.shape[1]
    block = rows // granules
    span = GMAX * block
    scale = width ** (-0.5)
    pick = jnp.where((iota((16, width), 0) == 0) & (iota((16, width), 1) == 0), 1.0, 0.0).astype(BF16)
    span_rows = iota((span, width), 0)
    span_lanes = iota((1, span), 1)
    for g in range(granules):
        pair = (first_ref[0, g] // granules) * 2 + (0 if g < granules // 2 else 1)
        filled = size_ref[0, g] * block
        raw = arrived_ref[pair]
        wide = raw.astype(F32)
        valid = (jnp.broadcast_to(wide[:, 0:1], wide.shape) < MARK_LIMIT) & (span_rows < filled)
        keys_ref[pl.ds(g * span, span), :] = jnp.where(valid, wide, 0.0).astype(BF16)
        q = nodes_ref[pl.ds(g * block, block), :]
        s = mm_nt(jnp.concatenate([q, pick], axis=0), raw)
        live_key = (s[block : block + 1, :] < MARK_LIMIT) & (span_lanes < filled)
        scores[pl.ds(g * block, block), :] = jnp.where(live_key, s[:block, :] * scale, -1e30)
    s = scores[...]
    powers = jnp.exp(s - jnp.max(s, axis=-1, keepdims=True))
    probs_ref[...] = powers / jnp.sum(powers, axis=-1, keepdims=True)
    for g in range(granules):
        at = pl.ds(g * block, block)
        context = mm(probs_ref[at, :].astype(BF16), keys_ref[pl.ds(g * span, span), :])
        moved[at, :] = (nodes_ref[at, :].astype(F32) - context).astype(BF16)

    chunk = 256
    per = chunk // block
    for k in range(rows // chunk):
        at = pl.ds(k * chunk, chunk)
        x = nodes_ref[at, :]
        hidden = (
            mm(x, w1_ref[:width, :])
            + mm(message_ref[at, :], w1_ref[width : 2 * width, :])
            + mm(moved[at, :], w1_ref[2 * width :, :])
            + b_ref[...]
        )
        s = sigmoid(hidden)
        act = (hidden * s).astype(BF16)
        active[at, :] = act
        mask = live_rows(live_ref, k * per, per, block, width)
        updated_ref[at, :] = jnp.where(
            mask, x.astype(F32) + mm(act, w2_ref[...]), 0.0
        ).astype(BF16)
        go = jnp.where(mask, cot_ref[at, :].astype(F32), 0.0)
        go_low = go.astype(BF16)
        out_grad[at, :] = go_low
        gh = (mm_nt(go_low, w2_ref[...]) * (s * (1.0 + hidden * (1.0 - s)))).astype(BF16)
        hidden_grad[at, :] = gh
        base_ref[at, :] = go + mm_nt(gh, w1_ref[:width, :])
        gmsg_ref[at, :] = mm_nt(gh, w1_ref[width : 2 * width, :]).astype(BF16)
        gmov_ref[at, :] = mm_nt(gh, w1_ref[2 * width :, :]).astype(BF16)
    gh = hidden_grad[...]
    bias_ref[...] = jnp.sum(gh.astype(F32), axis=0, keepdims=True)
    deal(stage, mm_tn(nodes_ref[...], gh), 0, 96, 0, 3, 0)
    deal(stage, mm_tn(message_ref[...], gh), width, 96, 0, 3, 0)
    deal(stage, mm_tn(moved[...], gh), 2 * width, 96, 0, 3, 0)
    deal(stage, mm_tn(active[...], out_grad[...]), 0, 64, 48, 3, 0)
    deal(stage, mm_tn(gathered_ref[...], gmsg_ref[...]), 0, 64, 64, 3, 0)
    for share in range(16, 32):
        for rep in range(8):
            stage[share, pl.ds((rep * 3 + 2) * 8, 8), :] = jnp.zeros((8, LANES), F32)
    send_ref[...] = stage[...].astype(BF16)


def edge_backward_kernel(
    src_ref, dst_ref, nodes_ref, w1_ref, w2_ref, slope_ref, gmsg_ref, base_ref, bias_ref,
    send_ref, total_ref,
    wide_grad, terms, grad_t, grad_s, col_t, stage,
):
    rows, width = nodes_ref.shape
    edges = src_ref.shape[1]
    chunk = 256
    col_t[...] = spread(dst_ref)
    for k in range(rows // chunk):
        at = pl.ds(k * chunk, chunk)
        wide_grad[at, :] = mm_nt(gmsg_ref[at, :], w2_ref[...]).astype(BF16)
    for k in range(edges // chunk):
        at = pl.ds(k * chunk, chunk)
        terms[at, :] = (
            mm(by_edge(col_t[at, :], rows), wide_grad[...]) * slope_ref[at, :].astype(F32)
        ).astype(BF16)
    column_sum = jnp.zeros((1, terms.shape[1]), F32)
    for k in range(rows // chunk):
        at = pl.ds(k * chunk, chunk)
        gt = mm(by_row(dst_ref, k * chunk, chunk), terms[...]).astype(BF16)
        gs = mm(by_row(src_ref, k * chunk, chunk), terms[...]).astype(BF16)
        grad_t[at, :] = gt
        grad_s[at, :] = gs
        column_sum = column_sum + jnp.sum(gt.astype(F32), axis=0, keepdims=True)
        total_ref[at, :] = (
            base_ref[at, :] + mm_nt(gt, w1_ref[:width, :]) + mm_nt(gs, w1_ref[width:, :])
        )
    x = nodes_ref[...]
    deal(stage, mm_tn(x, grad_t[...]), 0, 64, 0, 1, 0)
    deal(stage, mm_tn(x, grad_s[...]), width, 64, 0, 1, 0)
    both = jnp.concatenate([column_sum, bias_ref[...]], axis=1)
    tail = jnp.concatenate(
        [both[:, c * LANES : (c + 1) * LANES] for c in range(8)] + [jnp.zeros((8, LANES), F32)],
        axis=0,
    )
    for share in range(32):
        stage[share, pl.ds(64, 16), :] = tail
    send_ref[...] = stage[...].astype(BF16)


def attend_back_kernel(
    first_ref, nodes_ref, probs_ref, keys_ref, gmov_ref, base_ref,
    back_ref, total_ref,
    prob_grad,
):
    rows, width = nodes_ref.shape
    granules = first_ref.shape[1]
    block = rows // granules
    span = GMAX * block
    scale = width ** (-0.5)
    for g in range(granules):
        at = pl.ds(g * block, block)
        prob_grad[at, :] = -mm_nt(gmov_ref[at, :], keys_ref[pl.ds(g * span, span), :])
    probs = probs_ref[...]
    inner = jnp.sum(probs * prob_grad[...], axis=-1, keepdims=True)
    prob_grad[...] = probs * (prob_grad[...] - inner) * scale
    held = None
    for g in range(granules):
        at = pl.ds(g * block, block)
        pair = (first_ref[0, g] // granules) * 2 + (0 if g < granules // 2 else 1)
        gs = prob_grad[at, :].astype(BF16)
        gm = gmov_ref[at, :]
        total_ref[at, :] = (
            base_ref[at, :] + mm(gs, keys_ref[pl.ds(g * span, span), :]) + gm.astype(F32)
        )
        left = jnp.concatenate([probs_ref[at, :].astype(BF16), gs], axis=0)
        right = jnp.concatenate([-gm, nodes_ref[at, :]], axis=0)
        new = mm_tn(left, right)
        if held is None:
            held = new
        else:
            held = new + jnp.where(first_ref[0, g] == first_ref[0, g - 1], held, 0.0)
        back_ref[pair] = held.astype(BF16)


def finish_kernel(live_ref, first_ref, base_ref, back_ref, out_ref):
    granules, block, width = out_ref.shape
    rows = iota((block, width), 0)
    for g in range(granules):
        slot = (first_ref[0, g] // granules) * (2 * GMAX) + (GMAX if g < granules // 2 else 0)
        if g > 0:
            slot = slot + (first_ref[0, g] == first_ref[0, g - 1]).astype(jnp.int32)
        out_ref[g] = jnp.where(
            rows < live_ref[0, g],
            base_ref[pl.ds(g * block, block), :] + back_ref[slot].astype(F32),
            0.0,
        ).astype(BF16)


def collect(out_ref, wide, base, first_q, scale):
    rows, width = out_ref.shape
    across = width // LANES
    for i in range(rows // 8):
        for c in range(across):
            unit = base + i * across + c
            share, q = unit % 32, unit // 32 + first_q
            out_ref[pl.ds(8 * i, 8), pl.ds(c * LANES, LANES)] = (
                wide[share, pl.ds(8 * q, 8), :] * scale
            )


def unpack_kernel(scale, all_ref, e1_ref, e2_ref, n1_ref, n2_ref, wide):
    wide[...] = all_ref[...].astype(F32)
    collect(n1_ref, wide, 0, 0, scale)
    collect(n2_ref, wide, 48, 0, scale)
    collect(e2_ref, wide, 64, 0, scale)
    collect(e1_ref, wide, 0, 3, scale)


VM = pl.BlockSpec(memory_space=pltpu.VMEM)
SM = pl.BlockSpec(memory_space=pltpu.SMEM)


def call(kernel, name, in_specs, outs, scratch, *args):
    got = pl.pallas_call(
        kernel,
        name=name,
        out_shape=tuple(jax.ShapeDtypeStruct(s, d) for s, d in outs),
        in_specs=in_specs,
        out_specs=tuple(VM for _ in outs),
        scratch_shapes=[pltpu.VMEM(s, d) for s, d in scratch],
        compiler_params=pltpu.CompilerParams(vmem_limit_bytes=VMEM_LIMIT),
    )(*args)
    return got[0] if len(outs) == 1 else got


def exchange(x, axis):
    return lax.all_to_all(x, axis, split_axis=0, concat_axis=0, tiled=True)


def on_device(
    nodes, cotangent, live, partner_first, partner_size, edge_src, edge_dst,
    w_edge1, b_edge, w_edge2, w_node1, b_node, w_node2,
):
    granules, block, width = nodes.shape[1:]
    rows = granules * block
    edges = edge_src.shape[1]
    hidden = w_edge1.shape[1]
    peers, reps = lax.axis_size("graph"), lax.axis_size("rep")
    blocks = nodes[0]
    flat = blocks.reshape(rows, width)
    cot = cotangent[0].reshape(rows, width)
    slots = peers * 2 * GMAX
    span = GMAX * block

    outgoing = call(
        pack_kernel, "pack", [SM, SM, VM], (((slots, block, width), BF16),), [],
        live, partner_first, blocks,
    )
    arrived = exchange(outgoing, "graph").reshape(2 * peers, span, width)
    message, gathered, slope = call(
        edge_forward_kernel, "edge_forward", [VM] * 6,
        (((rows, width), BF16), ((rows, hidden), BF16), ((edges, hidden), BF16)),
        [
            ((rows, hidden), BF16), ((rows, hidden), BF16), ((edges, hidden), BF16),
            ((edges, LANES), jnp.int32), ((edges, LANES), jnp.int32),
        ],
        edge_src, edge_dst, flat, w_edge1, b_edge.reshape(1, hidden), w_edge2,
    )
    updated, probs, keys, grad_message, grad_moved, base, bias_node, node_send = call(
        node_kernel, "node", [SM, SM, SM] + [VM] * 8,
        (
            ((rows, width), BF16), ((rows, span), F32), ((granules * span, width), BF16),
            ((rows, width), BF16), ((rows, width), BF16), ((rows, width), F32),
            ((1, hidden), F32), ((peers, reps * 24, LANES), BF16),
        ),
        [
            ((rows, span), F32), ((rows, width), BF16), ((rows, hidden), BF16),
            ((rows, hidden), BF16), ((rows, width), BF16), ((peers, reps * 24, LANES), F32),
        ],
        live, partner_first, partner_size, flat, arrived, cot, message, gathered,
        w_node1, b_node.reshape(1, hidden), w_node2,
    )
    node_got = exchange(node_send, "graph")
    edge_send, base = call(
        edge_backward_kernel, "edge_backward", [VM] * 9,
        (((peers, reps * 8 + 16, LANES), BF16), ((rows, width), F32)),
        [
            ((rows, hidden), BF16), ((edges, hidden), BF16), ((rows, hidden), BF16),
            ((rows, hidden), BF16), ((edges, LANES), jnp.int32),
            ((peers, reps * 8 + 16, LANES), F32),
        ],
        edge_src, edge_dst, flat, w_edge1, w_edge2, slope, grad_message, base, bias_node,
    )
    edge_got = exchange(edge_send, "graph")
    back_send, base = call(
        attend_back_kernel, "attend_back", [SM] + [VM] * 5,
        (((2 * peers, span, width), BF16), ((rows, width), F32)),
        [((rows, span), F32)],
        partner_first, flat, probs, keys, grad_moved, base,
    )
    back_got = exchange(back_send.reshape(slots, block, width), "graph")

    node_sum = jnp.sum(node_got.astype(F32), axis=0).astype(BF16).reshape(reps, 24, LANES)
    edge_sum = jnp.sum(edge_got.astype(F32), axis=0).astype(BF16)
    second = jnp.concatenate(
        [
            node_sum,
            edge_sum[: reps * 8].reshape(reps, 8, LANES),
            jnp.broadcast_to(edge_sum[reps * 8 :][None], (reps, 16, LANES)),
        ],
        axis=1,
    )
    total = jnp.sum(exchange(second, "rep").astype(F32), axis=0)
    scale = (peers * reps * rows) ** (-0.5)
    third = jnp.broadcast_to(total[:32].astype(BF16)[None], (peers, 32, LANES))
    everything = exchange(third, "graph")
    share = hidden // reps
    biases = (total[32:40] * scale).reshape(2, hidden)
    start = lax.axis_index("rep") * share
    g_bedge = lax.dynamic_slice_in_dim(biases[0], start, share)
    g_bnode = lax.dynamic_slice_in_dim(biases[1], start, share)
    g_edge1, g_edge2, g_node1, g_node2 = call(
        functools.partial(unpack_kernel, scale), "unpack", [VM],
        (
            ((2 * width // reps, hidden), F32), ((hidden // reps, width), F32),
            ((3 * width // reps, hidden), F32), ((hidden // reps, width), F32),
        ),
        [((peers, 32, LANES), F32)],
        everything,
    )
    d_nodes = call(
        finish_kernel, "finish", [SM, SM, VM, VM], (((granules, block, width), BF16),), [],
        live, partner_first, base, back_got,
    )
    return (
        updated.reshape(1, granules, block, width),
        d_nodes.reshape(1, granules, block, width),
        g_edge1, g_bedge, g_edge2, g_node1, g_bnode, g_node2,
    )


def solution(mesh):
    placed = (P("rep", "graph", None, None),) * 2 + (P("rep", "graph"),) * 5 + (P(),) * 6
    return jax.shard_map(
        on_device,
        mesh=mesh,
        in_specs=placed,
        out_specs=(
            P("rep", "graph", None, None),
            P("rep", "graph", None, None),
            P("rep", None),
            P("rep"),
            P("rep", None),
            P("rep", None),
            P("rep"),
            P("rep", None),
        ),
        check_vma=False,
    )
```

```python
import functools

import jax
import jax.numpy as jnp
from jax import lax
from jax.experimental import pallas as pl
from jax.experimental.pallas import tpu as pltpu
from jax.sharding import PartitionSpec as P

F32 = jnp.float32
BF16 = jnp.bfloat16
GMAX = 2
LANES = 128
MARK = 16384.0
MARK_LIMIT = 8192.0
VMEM_LIMIT = 63 * 1024 * 1024
SMALL_LIMIT = 16 * 1024 * 1024


def mm(a, b):
    return jnp.dot(a, b, preferred_element_type=F32)


def mm_nt(a, b):
    return lax.dot_general(a, b, (((1,), (1,)), ((), ())), preferred_element_type=F32)


def mm_tn(a, b):
    return lax.dot_general(a, b, (((0,), (0,)), ((), ())), preferred_element_type=F32)


def sigmoid(v):
    return 1.0 / (1.0 + jnp.exp(-v))


def iota(shape, dim):
    return lax.broadcasted_iota(jnp.int32, shape, dim)


def live_rows(live_ref, first, count, block, width):
    limits = [jnp.full((block, width), live_ref[0, first + k], jnp.int32) for k in range(count)]
    positions = iota((block, width), 0)
    return jnp.concatenate([positions] * count, axis=0) < jnp.concatenate(limits, axis=0)


def one_hot(hit):
    return jnp.where(hit, 1.0, 0.0).astype(BF16)


def spread(row_ref):
    return jnp.transpose(jnp.broadcast_to(row_ref[...], (LANES, row_ref.shape[1])))


def by_edge(columns, rows):
    lanes = iota(columns.shape, 1)
    return jnp.concatenate(
        [one_hot(columns == lanes + k * LANES) for k in range(rows // LANES)], axis=1
    )


def by_row(row_ref, start, count):
    edges = row_ref.shape[1]
    return one_hot(
        jnp.broadcast_to(row_ref[...], (count, edges)) == iota((count, edges), 0) + start
    )


def pack_kernel(live_ref, first_ref, nodes_ref, out_ref, marked_ref, sems):
    granules, block, width = nodes_ref.shape
    rows, columns = iota((block, width), 0), iota((block, width), 1)
    copies = []
    for g in range(granules):
        slot = (first_ref[0, g] // granules) * (2 * GMAX) + (GMAX if g < granules // 2 else 0)
        if g > 0:
            slot = slot + (first_ref[0, g] == first_ref[0, g - 1]).astype(jnp.int32)
        marked = (rows >= live_ref[0, g]) & (columns == 0)
        marked_ref[g] = jnp.where(marked, MARK, nodes_ref[g].astype(F32)).astype(BF16)
        copy = pltpu.make_async_copy(marked_ref.at[g], out_ref.at[slot], sems.at[g])
        copy.start()
        copies.append(copy)
    for copy in copies:
        copy.wait()


def edge_forward_kernel(
    nodes_ref, w1_ref, b_ref, dst_ref, src_ref, w2_ref, live_ref, cot_ref, wn1_ref, bn_ref, wn2_ref,
    message_ref, gathered_ref, slope_ref, near_ref, lifted_ref,
    pre_t, pre_s, terms, col_t, col_s,
):
    rows, width = nodes_ref.shape
    edges = src_ref.shape[1]
    chunk = 256
    granules = live_ref.shape[1]
    block = rows // granules
    for k in range(rows // chunk):
        at = pl.ds(k * chunk, chunk)
        x = nodes_ref[at, :]
        pre_t[at, :] = (mm(x, w1_ref[:width, :]) + b_ref[...]).astype(BF16)
        pre_s[at, :] = mm(x, w1_ref[width:, :]).astype(BF16)
    col_t[...] = spread(dst_ref)
    col_s[...] = spread(src_ref)
    for k in range(edges // chunk):
        at = pl.ds(k * chunk, chunk)
        summed = mm(by_edge(col_t[at, :], rows), pre_t[...]) + mm(
            by_edge(col_s[at, :], rows), pre_s[...]
        )
        s = sigmoid(summed)
        terms[at, :] = (summed * s).astype(BF16)
        slope_ref[at, :] = (s * (1.0 + summed * (1.0 - s))).astype(BF16)
    for k in range(rows // chunk):
        at = pl.ds(k * chunk, chunk)
        gathered = mm(by_row(dst_ref, k * chunk, chunk), terms[...]).astype(BF16)
        gathered_ref[at, :] = gathered
        message = mm(gathered, w2_ref[...]).astype(BF16)
        message_ref[at, :] = message
        near_ref[at, :] = (
            mm(nodes_ref[at, :], wn1_ref[:width, :])
            + mm(message, wn1_ref[width : 2 * width, :])
            + bn_ref[...]
        )
        mask = live_rows(live_ref, k * (chunk // block), chunk // block, block, width)
        go = jnp.where(mask, cot_ref[at, :].astype(F32), 0.0).astype(BF16)
        lifted_ref[at, :] = mm_nt(go, wn2_ref[...])


def deal(stage, value, first_row, per_rep, base):
    rows, width = value.shape
    across = width // LANES
    for i in range(rows // 8):
        rep, inner = divmod(first_row + 8 * i, per_rep)
        for c in range(across):
            unit = base + (inner // 8) * across + c
            at = rep * 32 + unit % 32
            stage[at, pl.ds(unit // 32 * 8, 8), :] = value[
                8 * i : 8 * i + 8, c * LANES : (c + 1) * LANES
            ]


def main_kernel(
    live_ref, first_ref, size_ref, nodes_ref, arrived_ref, near_ref, wn1_ref, lifted_ref, wn2_ref,
    cot_ref, w2_ref, dst_ref, slope_ref, message_ref, src_ref, gathered_ref, w1_ref,
    probs_ref, keys_ref, gmov_ref, updated_ref, base_ref, send_ref,
    scores, moved, active, hidden_grad, out_grad, gmsg,
    wide_grad, terms, grad_t, grad_s, col_t, stage,
):
    rows, width = nodes_ref.shape
    granules = live_ref.shape[1]
    block = rows // granules
    span = GMAX * block
    scale = width ** (-0.5)
    pick = jnp.where((iota((16, width), 0) == 0) & (iota((16, width), 1) == 0), 1.0, 0.0).astype(BF16)
    span_rows = iota((span, width), 0)
    span_lanes = iota((1, span), 1)
    for g in range(granules):
        pair = (first_ref[0, g] // granules) * 2 + (0 if g < granules // 2 else 1)
        filled = size_ref[0, g] * block
        raw = arrived_ref[pair]
        wide = raw.astype(F32)
        valid = (jnp.broadcast_to(wide[:, 0:1], wide.shape) < MARK_LIMIT) & (span_rows < filled)
        keys_ref[pl.ds(g * span, span), :] = jnp.where(valid, wide, 0.0).astype(BF16)
        q = nodes_ref[pl.ds(g * block, block), :]
        s = mm_nt(jnp.concatenate([q, pick], axis=0), raw)
        live_key = (s[block : block + 1, :] < MARK_LIMIT) & (span_lanes < filled)
        scores[pl.ds(g * block, block), :] = jnp.where(live_key, s[:block, :] * scale, -1e30)
    keys_ref.flush()
    s = scores[...]
    powers = jnp.exp(s - jnp.max(s, axis=-1, keepdims=True))
    probs_ref[...] = powers / jnp.sum(powers, axis=-1, keepdims=True)
    probs_ref.flush()
    for g in range(granules):
        at = pl.ds(g * block, block)
        context = mm(probs_ref[at, :].astype(BF16), keys_ref[pl.ds(g * span, span), :])
        moved[at, :] = (nodes_ref[at, :].astype(F32) - context).astype(BF16)

    chunk = 256
    per = chunk // block
    for k in range(rows // chunk):
        at = pl.ds(k * chunk, chunk)
        hidden = near_ref[at, :] + mm(moved[at, :], wn1_ref[2 * width :, :])
        s = sigmoid(hidden)
        act = (hidden * s).astype(BF16)
        active[at, :] = act
        gh = (lifted_ref[at, :] * (s * (1.0 + hidden * (1.0 - s)))).astype(BF16)
        hidden_grad[at, :] = gh
        gm = mm_nt(gh, wn1_ref[width : 2 * width, :]).astype(BF16)
        gmsg[at, :] = gm
        gmov_ref[at, :] = mm_nt(gh, wn1_ref[2 * width :, :]).astype(BF16)
        wide_grad[at, :] = mm_nt(gm, w2_ref[...]).astype(BF16)
        mask = live_rows(live_ref, k * per, per, block, width)
        updated_ref[at, :] = jnp.where(
            mask, nodes_ref[at, :].astype(F32) + mm(act, wn2_ref[...]), 0.0
        ).astype(BF16)
        go = jnp.where(mask, cot_ref[at, :].astype(F32), 0.0)
        out_grad[at, :] = go.astype(BF16)
        base_ref[at, :] = go + mm_nt(gh, wn1_ref[:width, :])
    gmov_ref.flush()
    updated_ref.flush()
    gh = hidden_grad[...]
    node_bias = jnp.sum(gh.astype(F32), axis=0, keepdims=True)
    deal(stage, mm_tn(nodes_ref[...], gh), 0, 96, 0)
    deal(stage, mm_tn(moved[...], gh), 2 * width, 96, 0)
    deal(stage, mm_tn(active[...], out_grad[...]), 0, 64, 48)

    edges = src_ref.shape[1]
    col_t[...] = spread(dst_ref)
    for k in range(edges // chunk):
        at = pl.ds(k * chunk, chunk)
        terms[at, :] = (
            mm(by_edge(col_t[at, :], rows), wide_grad[...]) * slope_ref[at, :].astype(F32)
        ).astype(BF16)
    deal(stage, mm_tn(message_ref[...], gh), width, 96, 0)
    deal(stage, mm_tn(gathered_ref[...], gmsg[...]), 0, 64, 96)
    edge_bias = jnp.zeros((1, terms.shape[1]), F32)
    for k in range(rows // chunk):
        at = pl.ds(k * chunk, chunk)
        gt = mm(by_row(dst_ref, k * chunk, chunk), terms[...]).astype(BF16)
        gs = mm(by_row(src_ref, k * chunk, chunk), terms[...]).astype(BF16)
        grad_t[at, :] = gt
        grad_s[at, :] = gs
        edge_bias = edge_bias + jnp.sum(gt.astype(F32), axis=0, keepdims=True)
        base_ref[at, :] = (
            base_ref[at, :] + mm_nt(gt, w1_ref[:width, :]) + mm_nt(gs, w1_ref[width:, :])
        )
    base_ref.flush()
    x = nodes_ref[...]
    deal(stage, mm_tn(x, grad_t[...]), 0, 64, 64)
    deal(stage, mm_tn(x, grad_s[...]), width, 64, 64)
    biases = jnp.concatenate(
        [edge_bias, node_bias, jnp.zeros((6, edge_bias.shape[1]), F32)], axis=0
    )
    for rep in range(8):
        piece = biases[:, rep // 2 * LANES : (rep // 2 + 1) * LANES]
        for share in range(16, 32):
            stage[rep * 32 + share, pl.ds(24, 8), :] = piece
    send_ref[...] = stage[...].astype(BF16)


def attend_back_kernel(
    first_ref, nodes_ref, probs_ref, keys_ref, gmov_ref, base_ref,
    back_ref, total_ref,
    prob_grad,
):
    rows, width = nodes_ref.shape
    granules = first_ref.shape[1]
    block = rows // granules
    span = GMAX * block
    scale = width ** (-0.5)
    for g in range(granules):
        at = pl.ds(g * block, block)
        prob_grad[at, :] = -mm_nt(gmov_ref[at, :], keys_ref[pl.ds(g * span, span), :])
    probs = probs_ref[...]
    inner = jnp.sum(probs * prob_grad[...], axis=-1, keepdims=True)
    prob_grad[...] = probs * (prob_grad[...] - inner) * scale
    held = None
    for g in range(granules):
        at = pl.ds(g * block, block)
        pair = (first_ref[0, g] // granules) * 2 + (0 if g < granules // 2 else 1)
        gs = prob_grad[at, :].astype(BF16)
        gm = gmov_ref[at, :]
        total_ref[at, :] = (
            base_ref[at, :] + mm(gs, keys_ref[pl.ds(g * span, span), :]) + gm.astype(F32)
        )
        left = jnp.concatenate([probs_ref[at, :].astype(BF16), gs], axis=0)
        right = jnp.concatenate([-gm, nodes_ref[at, :]], axis=0)
        new = mm_tn(left, right)
        if held is None:
            held = new
        else:
            held = new + jnp.where(first_ref[0, g] == first_ref[0, g - 1], held, 0.0)
        back_ref[pair] = held.astype(BF16)


def finish_kernel(live_ref, first_ref, base_ref, back_ref, out_ref):
    granules, block, width = out_ref.shape
    rows = iota((block, width), 0)
    for g in range(granules):
        slot = (first_ref[0, g] // granules) * (2 * GMAX) + (GMAX if g < granules // 2 else 0)
        if g > 0:
            slot = slot + (first_ref[0, g] == first_ref[0, g - 1]).astype(jnp.int32)
        out_ref[g] = jnp.where(
            rows < live_ref[0, g],
            base_ref[pl.ds(g * block, block), :] + back_ref[slot].astype(F32),
            0.0,
        ).astype(BF16)


def share_sum_kernel(got_ref, out_ref):
    total = got_ref[0].astype(F32)
    for k in range(1, got_ref.shape[0]):
        total = total + got_ref[k].astype(F32)
    low = total.astype(BF16)
    for k in range(out_ref.shape[0]):
        out_ref[k] = low


def collect(out_ref, wide, base, scale):
    rows, width = out_ref.shape
    across = width // LANES
    for i in range(rows // 8):
        for c in range(across):
            unit = base + i * across + c
            out_ref[pl.ds(8 * i, 8), pl.ds(c * LANES, LANES)] = (
                wide[unit % 32, pl.ds(unit // 32 * 8, 8), :] * scale
            )


def unpack_kernel(scale, all_ref, e1_ref, be_ref, e2_ref, n1_ref, bn_ref, n2_ref, wide):
    wide[...] = all_ref[...].astype(F32)
    collect(n1_ref, wide, 0, scale)
    collect(n2_ref, wide, 48, scale)
    collect(e1_ref, wide, 64, scale)
    collect(e2_ref, wide, 96, scale)
    biases = wide[16, pl.ds(24, 8), :] * scale
    half = LANES // 2
    piece = jnp.where(lax.rem(lax.axis_index("rep"), 2) == 0, biases[:, :half], biases[:, half:])
    be_ref[...] = piece[0:1, :]
    bn_ref[...] = piece[1:2, :]


class Fetched:
    def __init__(self, ref, copy):
        self.ref, self.copy, self.shape, self.ready = ref, copy, ref.shape, False

    def wait(self):
        if not self.ready:
            self.copy.wait()
            self.ready = True
        return self.ref

    def __getitem__(self, at):
        return self.wait()[at]


class Written:
    def __init__(self, ref, copy):
        self.ref, self.copy, self.shape, self.sent = ref, copy, ref.shape, False

    def __setitem__(self, at, value):
        self.ref[at] = value

    def __getitem__(self, at):
        return self.ref[at]

    def flush(self):
        self.copy.start()
        self.sent = True


HB = pl.BlockSpec(memory_space=pltpu.HBM)
SMALL, WIDE, RAW = 0, 1, 2


def call(kernel, name, kinds, outs, scratch, *args, raw_out=False, limit=VMEM_LIMIT):
    fetched = [k for k, kind in enumerate(kinds) if kind != RAW]
    n_in, n_out = len(args), len(outs)

    def body(*refs):
        ins, results = refs[:n_in], refs[n_in : n_in + n_out]
        rest = list(refs[n_in + n_out :])
        in_sem, out_sem = rest.pop(0), rest.pop(0)
        given = list(ins)
        for at, k in enumerate(fetched):
            copy = pltpu.make_async_copy(ins[k], rest[at], in_sem.at[at])
            copy.start()
            given[k] = Fetched(rest[at], copy)
        rest = rest[len(fetched) :]
        if raw_out:
            written = list(results)
        else:
            written = [
                Written(rest[k], pltpu.make_async_copy(rest[k], results[k], out_sem.at[k]))
                for k in range(n_out)
            ]
            rest = rest[n_out:]
        kernel(*given, *written, *rest)
        for one in given:
            if isinstance(one, Fetched):
                one.wait()
        if not raw_out:
            for one in written:
                if not one.sent:
                    one.flush()
            for one in written:
                one.copy.wait()

    buffers = [
        (pltpu.SMEM if kinds[k] == SMALL else pltpu.VMEM)(args[k].shape, args[k].dtype)
        for k in fetched
    ]
    if not raw_out:
        buffers += [pltpu.VMEM(s, d) for s, d in outs]
    got = pl.pallas_call(
        body,
        name=name,
        out_shape=tuple(jax.ShapeDtypeStruct(s, d) for s, d in outs),
        in_specs=[HB] * n_in,
        out_specs=(HB,) * n_out,
        scratch_shapes=[
            pltpu.SemaphoreType.DMA((max(len(fetched), 1),)),
            pltpu.SemaphoreType.DMA((n_out,)),
            *buffers,
            *[s if not isinstance(s, tuple) else pltpu.VMEM(*s) for s in scratch],
        ],
        compiler_params=pltpu.CompilerParams(vmem_limit_bytes=limit),
    )(*args)
    return got[0] if n_out == 1 else got


def exchange(x, axis):
    return lax.all_to_all(x, axis, split_axis=0, concat_axis=0, tiled=True)


def on_device(
    nodes, cotangent, live, partner_first, partner_size, edge_src, edge_dst,
    w_edge1, b_edge, w_edge2, w_node1, b_node, w_node2,
):
    granules, block, width = nodes.shape[1:]
    rows = granules * block
    edges = edge_src.shape[1]
    hidden = w_edge1.shape[1]
    peers, reps = lax.axis_size("graph"), lax.axis_size("rep")
    blocks = nodes[0]
    flat = blocks.reshape(rows, width)
    cot = cotangent[0].reshape(rows, width)
    slots = peers * 2 * GMAX
    span = GMAX * block

    outgoing = call(
        pack_kernel, "pack", [SMALL, SMALL, WIDE], (((slots, block, width), BF16),),
        [((granules, block, width), BF16), pltpu.SemaphoreType.DMA((granules,))],
        live, partner_first, blocks, raw_out=True,
    )
    arrived = exchange(outgoing, "graph").reshape(2 * peers, span, width)
    message, gathered, slope, near, lifted = call(
        edge_forward_kernel, "edge_forward", [WIDE] * 6 + [SMALL] + [WIDE] * 4,
        (
            ((rows, width), BF16), ((rows, hidden), BF16), ((edges, hidden), BF16),
            ((rows, hidden), F32), ((rows, hidden), F32),
        ),
        [
            ((rows, hidden), BF16), ((rows, hidden), BF16), ((edges, hidden), BF16),
            ((edges, LANES), jnp.int32), ((edges, LANES), jnp.int32),
        ],
        flat, w_edge1, b_edge.reshape(1, hidden), edge_dst, edge_src, w_edge2,
        live, cot, w_node1, b_node.reshape(1, hidden), w_node2,
    )
    probs, keys, grad_moved, updated, base, send = call(
        main_kernel, "main", [SMALL] * 3 + [WIDE] * 14,
        (
            ((rows, span), F32), ((granules * span, width), BF16), ((rows, width), BF16),
            ((rows, width), BF16), ((rows, width), F32), ((reps * peers, 32, LANES), BF16),
        ),
        [
            ((rows, span), F32), ((rows, width), BF16), ((rows, hidden), BF16),
            ((rows, hidden), BF16), ((rows, width), BF16), ((rows, width), BF16),
            ((rows, hidden), BF16), ((edges, hidden), BF16), ((rows, hidden), BF16),
            ((rows, hidden), BF16), ((edges, LANES), jnp.int32),
            ((reps * peers, 32, LANES), F32),
        ],
        live, partner_first, partner_size, flat, arrived, near, w_node1, lifted, w_node2,
        cot, w_edge2, edge_dst, slope, message, edge_src, gathered, w_edge1,
    )
    part = lax.psum_scatter(send, "rep", scatter_dimension=0, tiled=True)
    back_send, base = call(
        attend_back_kernel, "attend_back", [SMALL] + [WIDE] * 5,
        (((2 * peers, span, width), BF16), ((rows, width), F32)),
        [((rows, span), F32)],
        partner_first, flat, probs, keys, grad_moved, base,
    )
    back_got = exchange(back_send.reshape(slots, block, width), "graph")
    part, back_got = lax.optimization_barrier((part, back_got))
    everything = exchange(
        call(
            share_sum_kernel, "share_sum", [WIDE], (((peers, 32, LANES), BF16),), [],
            exchange(part, "graph"), limit=SMALL_LIMIT,
        ),
        "graph",
    )
    scale = (peers * reps * rows) ** (-0.5)
    share = hidden // reps
    g_edge1, g_bedge, g_edge2, g_node1, g_bnode, g_node2 = call(
        functools.partial(unpack_kernel, scale), "unpack", [WIDE],
        (
            ((2 * width // reps, hidden), F32), ((1, share), F32), ((share, width), F32),
            ((3 * width // reps, hidden), F32), ((1, share), F32), ((share, width), F32),
        ),
        [((peers, 32, LANES), F32)],
        everything, limit=SMALL_LIMIT,
    )
    d_nodes = call(
        finish_kernel, "finish", [SMALL, SMALL, WIDE, WIDE], (((granules, block, width), BF16),), [],
        live, partner_first, base, back_got,
    )
    return (
        updated.reshape(1, granules, block, width),
        d_nodes.reshape(1, granules, block, width),
        g_edge1, g_bedge.reshape(share), g_edge2, g_node1, g_bnode.reshape(share), g_node2,
    )


def solution(mesh):
    placed = (P("rep", "graph", None, None),) * 2 + (P("rep", "graph"),) * 5 + (P(),) * 6
    return jax.shard_map(
        on_device,
        mesh=mesh,
        in_specs=placed,
        out_specs=(
            P("rep", "graph", None, None),
            P("rep", "graph", None, None),
            P("rep", None),
            P("rep"),
            P("rep", None),
            P("rep", None),
            P("rep"),
            P("rep", None),
        ),
        check_vma=False,
    )
```

```python
import functools

import jax
import jax.numpy as jnp
from jax import lax
from jax.experimental import pallas as pl
from jax.experimental.pallas import tpu as pltpu
from jax.sharding import PartitionSpec as P

F32 = jnp.float32
BF16 = jnp.bfloat16
GMAX = 2
LANES = 128
MARK = 16384.0
MARK_LIMIT = 8192.0
VMEM_LIMIT = 63 * 1024 * 1024
SMALL_LIMIT = 16 * 1024 * 1024


def mm(a, b):
    return jnp.dot(a, b, preferred_element_type=F32)


def mm_nt(a, b):
    return lax.dot_general(a, b, (((1,), (1,)), ((), ())), preferred_element_type=F32)


def mm_tn(a, b):
    return lax.dot_general(a, b, (((0,), (0,)), ((), ())), preferred_element_type=F32)


def sigmoid(v):
    return 1.0 / (1.0 + jnp.exp(-v))


def iota(shape, dim):
    return lax.broadcasted_iota(jnp.int32, shape, dim)


def live_rows(live_ref, first, count, block, width):
    limits = [jnp.full((block, width), live_ref[0, first + k], jnp.int32) for k in range(count)]
    positions = iota((block, width), 0)
    return jnp.concatenate([positions] * count, axis=0) < jnp.concatenate(limits, axis=0)


def one_hot(hit):
    return jnp.where(hit, 1.0, 0.0).astype(BF16)


def spread(row_ref):
    return jnp.transpose(jnp.broadcast_to(row_ref[...], (LANES, row_ref.shape[1])))


def flipped(x):
    return jnp.transpose(x.astype(F32)).astype(BF16)


def by_edge(columns, rows):
    lanes = iota(columns.shape, 1)
    return jnp.concatenate(
        [one_hot(columns == lanes + k * LANES) for k in range(rows // LANES)], axis=1
    )


def by_row(row_ref, start, count):
    edges = row_ref.shape[1]
    return one_hot(
        jnp.broadcast_to(row_ref[...], (count, edges)) == iota((count, edges), 0) + start
    )


def pack_kernel(live_ref, first_ref, nodes_ref, out_ref, marked_ref, sems):
    granules, block, width = nodes_ref.shape
    rows, columns = iota((block, width), 0), iota((block, width), 1)
    copies = []
    for g in range(granules):
        slot = (first_ref[0, g] // granules) * (2 * GMAX) + (GMAX if g < granules // 2 else 0)
        if g > 0:
            slot = slot + (first_ref[0, g] == first_ref[0, g - 1]).astype(jnp.int32)
        marked = (rows >= live_ref[0, g]) & (columns == 0)
        marked_ref[g] = jnp.where(marked, MARK, nodes_ref[g].astype(F32)).astype(BF16)
        copy = pltpu.make_async_copy(marked_ref.at[g], out_ref.at[slot], sems.at[g])
        copy.start()
        copies.append(copy)
    for copy in copies:
        copy.wait()


def edge_forward_kernel(
    nodes_ref, w1_ref, b_ref, dst_ref, src_ref, w2_ref, live_ref, cot_ref, wn1_ref, bn_ref, wn2_ref,
    flip_ref, slope_ref, near_ref, lifted_ref,
    pre_t, pre_s, terms, col_t, col_s,
):
    rows, width = nodes_ref.shape
    edges = src_ref.shape[1]
    chunk = 256
    granules = live_ref.shape[1]
    block = rows // granules
    for k in range(rows // chunk):
        at = pl.ds(k * chunk, chunk)
        x = nodes_ref[at, :]
        pre_t[at, :] = (mm(x, w1_ref[:width, :]) + b_ref[...]).astype(BF16)
        pre_s[at, :] = mm(x, w1_ref[width:, :]).astype(BF16)
    col_t[...] = spread(dst_ref)
    col_s[...] = spread(src_ref)
    for k in range(edges // chunk):
        at = pl.ds(k * chunk, chunk)
        summed = mm(by_edge(col_t[at, :], rows), pre_t[...]) + mm(
            by_edge(col_s[at, :], rows), pre_s[...]
        )
        s = sigmoid(summed)
        terms[at, :] = (summed * s).astype(BF16)
        slope_ref[at, :] = (s * (1.0 + summed * (1.0 - s))).astype(BF16)
    for k in range(rows // chunk):
        at = pl.ds(k * chunk, chunk)
        gathered = mm(by_row(dst_ref, k * chunk, chunk), terms[...]).astype(BF16)
        message = mm(gathered, w2_ref[...]).astype(BF16)
        flip_ref[pl.ds(0, width), at] = flipped(nodes_ref[at, :])
        flip_ref[pl.ds(width, width), at] = flipped(message)
        flip_ref[pl.ds(2 * width, gathered.shape[1]), at] = flipped(gathered)
        near_ref[at, :] = (
            mm(nodes_ref[at, :], wn1_ref[:width, :])
            + mm(message, wn1_ref[width : 2 * width, :])
            + bn_ref[...]
        )
        mask = live_rows(live_ref, k * (chunk // block), chunk // block, block, width)
        go = jnp.where(mask, cot_ref[at, :].astype(F32), 0.0).astype(BF16)
        lifted_ref[at, :] = mm_nt(go, wn2_ref[...])


def deal(stage, value, first_row, per_rep, base):
    rows, width = value.shape
    across = width // LANES
    for i in range(rows // 8):
        rep, inner = divmod(first_row + 8 * i, per_rep)
        for c in range(across):
            unit = base + (inner // 8) * across + c
            at = rep * 32 + unit % 32
            stage[at, pl.ds(unit // 32 * 8, 8), :] = value[
                8 * i : 8 * i + 8, c * LANES : (c + 1) * LANES
            ]


def main_kernel(
    live_ref, first_ref, size_ref, nodes_ref, arrived_ref, near_ref, wn1_ref, lifted_ref,
    w2_ref, cot_ref, flip_ref, dst_ref, slope_ref, src_ref,
    probs_ref, keys_ref, gmov_ref, active, hidden_grad, grad_t, grad_s, send_ref,
    scores, moved, out_grad, gmsg, wide_grad, terms, col_t, stage, row_sems, send_sems,
):
    rows, width = nodes_ref.shape
    granules = live_ref.shape[1]
    block = rows // granules
    span = GMAX * block
    scale = width ** (-0.5)
    pick = jnp.where((iota((16, width), 0) == 0) & (iota((16, width), 1) == 0), 1.0, 0.0).astype(BF16)
    span_rows = iota((span, width), 0)
    span_lanes = iota((1, span), 1)
    arrived_ref.wait()
    for later in (near_ref, wn1_ref, lifted_ref, w2_ref, cot_ref):
        later.start()
    for g in range(granules):
        pair = (first_ref[0, g] // granules) * 2 + (0 if g < granules // 2 else 1)
        filled = size_ref[0, g] * block
        raw = arrived_ref[pair]
        wide = raw.astype(F32)
        valid = (jnp.broadcast_to(wide[:, 0:1], wide.shape) < MARK_LIMIT) & (span_rows < filled)
        keys_ref[pl.ds(g * span, span), :] = jnp.where(valid, wide, 0.0).astype(BF16)
        q = nodes_ref[pl.ds(g * block, block), :]
        s = mm_nt(jnp.concatenate([q, pick], axis=0), raw)
        live_key = (s[block : block + 1, :] < MARK_LIMIT) & (span_lanes < filled)
        scores[pl.ds(g * block, block), :] = jnp.where(live_key, s[:block, :] * scale, -1e30)
    keys_ref.flush()
    for later in (flip_ref, dst_ref, slope_ref, src_ref):
        later.start()
    s = scores[...]
    powers = jnp.exp(s - jnp.max(s, axis=-1, keepdims=True))
    probs_ref[...] = powers / jnp.sum(powers, axis=-1, keepdims=True)
    probs_ref.flush()
    for g in range(granules):
        at = pl.ds(g * block, block)
        context = mm(probs_ref[at, :].astype(BF16), keys_ref[pl.ds(g * span, span), :])
        moved[at, :] = (nodes_ref[at, :].astype(F32) - context).astype(BF16)

    chunk = 256
    per = chunk // block
    for k in range(rows // chunk):
        at = pl.ds(k * chunk, chunk)
        hidden = near_ref[at, :] + mm(moved[at, :], wn1_ref[2 * width :, :])
        s = sigmoid(hidden)
        act = (hidden * s).astype(BF16)
        active[at, :] = act
        gh = (lifted_ref[at, :] * (s * (1.0 + hidden * (1.0 - s)))).astype(BF16)
        hidden_grad[at, :] = gh
        gm = mm_nt(gh, wn1_ref[width : 2 * width, :]).astype(BF16)
        gmsg[at, :] = gm
        gmov_ref[at, :] = mm_nt(gh, wn1_ref[2 * width :, :]).astype(BF16)
        wide_grad[at, :] = mm_nt(gm, w2_ref[...]).astype(BF16)
        mask = live_rows(live_ref, k * per, per, block, width)
        out_grad[at, :] = jnp.where(mask, cot_ref[at, :].astype(F32), 0.0).astype(BF16)
    gmov_ref.flush()
    active.flush()
    hidden_grad.flush()
    gh = hidden_grad[...]
    node_bias = jnp.sum(gh.astype(F32), axis=0, keepdims=True)
    deal(stage, mm(flip_ref[pl.ds(0, 2 * width), :], gh), 0, 96, 0)
    deal(stage, mm_tn(moved[...], gh), 2 * width, 96, 0)
    deal(stage, mm_tn(active[...], out_grad[...]), 0, 64, 48)

    edges = src_ref.shape[1]
    col_t[...] = spread(dst_ref)
    for k in range(edges // chunk):
        at = pl.ds(k * chunk, chunk)
        terms[at, :] = (
            mm(by_edge(col_t[at, :], rows), wide_grad[...]) * slope_ref[at, :].astype(F32)
        ).astype(BF16)
    deal(stage, mm(flip_ref[pl.ds(2 * width, gh.shape[1]), :], gmsg[...]), 0, 64, 96)
    cuts = [(pl.ds(0, 256), pl.ds(0, 16)), (pl.ds(0, 128), pl.ds(16, 16)), (pl.ds(128, 128), pl.ds(16, 16))]
    sends = send_ref.pieces(cuts, send_sems)
    send_ref[:, pl.ds(0, 16), :] = stage[:, pl.ds(0, 16), :].astype(BF16)
    sends[0].start()
    row_cuts = [(pl.ds(k * chunk, chunk),) for k in range(rows // chunk)]
    rows_t = grad_t.pieces(row_cuts, row_sems.at[0])
    rows_s = grad_s.pieces(row_cuts, row_sems.at[1])
    edge_bias = jnp.zeros((1, terms.shape[1]), F32)
    for k in range(rows // chunk):
        at = pl.ds(k * chunk, chunk)
        gt = mm(by_row(dst_ref, k * chunk, chunk), terms[...]).astype(BF16)
        gs = mm(by_row(src_ref, k * chunk, chunk), terms[...]).astype(BF16)
        grad_t[at, :] = gt
        grad_s[at, :] = gs
        edge_bias = edge_bias + jnp.sum(gt.astype(F32), axis=0, keepdims=True)
        rows_t[k].start()
        rows_s[k].start()
    biases = jnp.concatenate(
        [edge_bias, node_bias, jnp.zeros((6, edge_bias.shape[1]), F32)], axis=0
    )
    for rep in range(8):
        piece = biases[:, rep // 2 * LANES : (rep // 2 + 1) * LANES]
        for share in range(16, 32):
            stage[rep * 32 + share, pl.ds(24, 8), :] = piece
    x = flip_ref[pl.ds(0, width), :]
    for half, grad in enumerate((grad_t, grad_s)):
        deal(stage, mm(x, grad[...]), half * width, 64, 64)
        at = pl.ds(half * 128, 128)
        send_ref[at, pl.ds(16, 16), :] = stage[at, pl.ds(16, 16), :].astype(BF16)
        sends[1 + half].start()


def attend_back_kernel(
    first_ref, gmov_ref, keys_ref, probs_ref, nodes_ref,
    back_ref, gscores_ref,
    prob_grad,
):
    rows, width = nodes_ref.shape
    granules = first_ref.shape[1]
    block = rows // granules
    span = GMAX * block
    scale = width ** (-0.5)
    for g in range(granules):
        at = pl.ds(g * block, block)
        prob_grad[at, :] = -mm_nt(gmov_ref[at, :], keys_ref[pl.ds(g * span, span), :])
    probs = probs_ref[...]
    inner = jnp.sum(probs * prob_grad[...], axis=-1, keepdims=True)
    gscores_ref[...] = (probs * (prob_grad[...] - inner) * scale).astype(BF16)
    gscores_ref.flush()
    held = None
    for g in range(granules):
        at = pl.ds(g * block, block)
        pair = (first_ref[0, g] // granules) * 2 + (0 if g < granules // 2 else 1)
        left = jnp.concatenate([probs_ref[at, :].astype(BF16), gscores_ref[at, :]], axis=0)
        right = jnp.concatenate([-gmov_ref[at, :], nodes_ref[at, :]], axis=0)
        new = mm_tn(left, right)
        if held is None:
            held = new
        else:
            held = new + jnp.where(first_ref[0, g] == first_ref[0, g - 1], held, 0.0)
        back_ref[pair] = held.astype(BF16)


def finish_kernel(
    live_ref, first_ref, active, hidden_grad, wn2_ref, wn1_ref, nodes_ref, grad_t, grad_s, w1_ref,
    gscores_ref, keys_ref, gmov_ref, cot_ref, back_ref,
    updated_ref, out_ref,
    base,
):
    rows, width = nodes_ref.shape
    granules = live_ref.shape[1]
    block = rows // granules
    span = GMAX * block
    chunk = 256
    per = chunk // block
    for k in range(rows // chunk):
        at = pl.ds(k * chunk, chunk)
        mask = live_rows(live_ref, k * per, per, block, width)
        updated_ref[at, :] = jnp.where(
            mask, nodes_ref[at, :].astype(F32) + mm(active[at, :], wn2_ref[...]), 0.0
        ).astype(BF16)
        base[at, :] = (
            mm_nt(hidden_grad[at, :], wn1_ref[:width, :])
            + mm_nt(grad_t[at, :], w1_ref[:width, :])
            + mm_nt(grad_s[at, :], w1_ref[width:, :])
        )
    updated_ref.flush()
    positions = iota((block, width), 0)
    for g in range(granules):
        at = pl.ds(g * block, block)
        slot = (first_ref[0, g] // granules) * (2 * GMAX) + (GMAX if g < granules // 2 else 0)
        if g > 0:
            slot = slot + (first_ref[0, g] == first_ref[0, g - 1]).astype(jnp.int32)
        total = (
            base[at, :]
            + cot_ref[at, :].astype(F32)
            + gmov_ref[at, :].astype(F32)
            + mm(gscores_ref[at, :], keys_ref[pl.ds(g * span, span), :])
            + back_ref[slot].astype(F32)
        )
        out_ref[at, :] = jnp.where(positions < live_ref[0, g], total, 0.0).astype(BF16)


def share_sum_kernel(got_ref, out_ref):
    total = got_ref[0].astype(F32)
    for k in range(1, got_ref.shape[0]):
        total = total + got_ref[k].astype(F32)
    low = total.astype(BF16)
    for k in range(out_ref.shape[0]):
        out_ref[k] = low


def collect(out_ref, wide, base, scale):
    rows, width = out_ref.shape
    across = width // LANES
    for i in range(rows // 8):
        for c in range(across):
            unit = base + i * across + c
            out_ref[pl.ds(8 * i, 8), pl.ds(c * LANES, LANES)] = (
                wide[unit % 32, pl.ds(unit // 32 * 8, 8), :] * scale
            )


def unpack_kernel(scale, all_ref, e1_ref, be_ref, e2_ref, n1_ref, bn_ref, n2_ref, wide):
    wide[...] = all_ref[...].astype(F32)
    collect(n1_ref, wide, 0, scale)
    collect(n2_ref, wide, 48, scale)
    collect(e1_ref, wide, 64, scale)
    collect(e2_ref, wide, 96, scale)
    biases = wide[16, pl.ds(24, 8), :] * scale
    half = LANES // 2
    piece = jnp.where(lax.rem(lax.axis_index("rep"), 2) == 0, biases[:, :half], biases[:, half:])
    be_ref[...] = piece[0:1, :]
    bn_ref[...] = piece[1:2, :]


class Fetched:
    def __init__(self, ref, copy):
        self.ref, self.copy, self.shape = ref, copy, ref.shape
        self.started = self.ready = False

    def start(self):
        if not self.started:
            self.copy.start()
            self.started = True

    def wait(self):
        self.start()
        if not self.ready:
            self.copy.wait()
            self.ready = True
        return self.ref

    def __getitem__(self, at):
        return self.wait()[at]


class Written:
    def __init__(self, ref, out, copy):
        self.ref, self.out, self.copy, self.shape, self.sent = ref, out, copy, ref.shape, False

    def __setitem__(self, at, value):
        self.ref[at] = value

    def __getitem__(self, at):
        return self.ref[at]

    def flush(self):
        self.copy.start()
        self.sent = True

    def pieces(self, cuts, sems):
        self.sent = True
        self.copy = Many(
            [pltpu.make_async_copy(self.ref.at[c], self.out.at[c], sems.at[k]) for k, c in enumerate(cuts)]
        )
        return self.copy.copies


class Many:
    def __init__(self, copies):
        self.copies = copies

    def wait(self):
        for copy in self.copies:
            copy.wait()


HB = pl.BlockSpec(memory_space=pltpu.HBM)
SMALL, WIDE, RAW = 0, 1, 2


def call(kernel, name, kinds, outs, scratch, *args, raw_out=False, limit=VMEM_LIMIT, eager=99):
    fetched = [k for k, kind in enumerate(kinds) if kind != RAW]
    n_in, n_out = len(args), len(outs)

    def body(*refs):
        ins, results = refs[:n_in], refs[n_in : n_in + n_out]
        rest = list(refs[n_in + n_out :])
        in_sem, out_sem = rest.pop(0), rest.pop(0)
        given = list(ins)
        for at, k in enumerate(fetched):
            copy = pltpu.make_async_copy(ins[k], rest[at], in_sem.at[at])
            given[k] = Fetched(rest[at], copy)
            if k < eager:
                given[k].start()
        rest = rest[len(fetched) :]
        if raw_out:
            written = list(results)
        else:
            written = [
                Written(
                    rest[k], results[k], pltpu.make_async_copy(rest[k], results[k], out_sem.at[k])
                )
                for k in range(n_out)
            ]
            rest = rest[n_out:]
        kernel(*given, *written, *rest)
        for one in given:
            if isinstance(one, Fetched):
                one.wait()
        if not raw_out:
            for one in written:
                if not one.sent:
                    one.flush()
            for one in written:
                one.copy.wait()

    buffers = [
        (pltpu.SMEM if kinds[k] == SMALL else pltpu.VMEM)(args[k].shape, args[k].dtype)
        for k in fetched
    ]
    if not raw_out:
        buffers += [pltpu.VMEM(s, d) for s, d in outs]
    got = pl.pallas_call(
        body,
        name=name,
        out_shape=tuple(jax.ShapeDtypeStruct(s, d) for s, d in outs),
        in_specs=[HB] * n_in,
        out_specs=(HB,) * n_out,
        scratch_shapes=[
            pltpu.SemaphoreType.DMA((max(len(fetched), 1),)),
            pltpu.SemaphoreType.DMA((n_out,)),
            *buffers,
            *[s if not isinstance(s, tuple) else pltpu.VMEM(*s) for s in scratch],
        ],
        compiler_params=pltpu.CompilerParams(vmem_limit_bytes=limit),
    )(*args)
    return got[0] if n_out == 1 else got


def exchange(x, axis):
    return lax.all_to_all(x, axis, split_axis=0, concat_axis=0, tiled=True)


def on_device(
    nodes, cotangent, live, partner_first, partner_size, edge_src, edge_dst,
    w_edge1, b_edge, w_edge2, w_node1, b_node, w_node2,
):
    granules, block, width = nodes.shape[1:]
    rows = granules * block
    edges = edge_src.shape[1]
    hidden = w_edge1.shape[1]
    peers, reps = lax.axis_size("graph"), lax.axis_size("rep")
    blocks = nodes[0]
    flat = blocks.reshape(rows, width)
    cot = cotangent[0].reshape(rows, width)
    slots = peers * 2 * GMAX
    span = GMAX * block

    outgoing = call(
        pack_kernel, "pack", [SMALL, SMALL, WIDE], (((slots, block, width), BF16),),
        [((granules, block, width), BF16), pltpu.SemaphoreType.DMA((granules,))],
        live, partner_first, blocks, raw_out=True,
    )
    arrived = exchange(outgoing, "graph").reshape(2 * peers, span, width)
    flip, slope, near, lifted = call(
        edge_forward_kernel, "edge_forward", [WIDE] * 6 + [SMALL] + [WIDE] * 4,
        (
            ((2 * width + hidden, rows), BF16), ((edges, hidden), BF16),
            ((rows, hidden), F32), ((rows, hidden), F32),
        ),
        [
            ((rows, hidden), BF16), ((rows, hidden), BF16), ((edges, hidden), BF16),
            ((edges, LANES), jnp.int32), ((edges, LANES), jnp.int32),
        ],
        flat, w_edge1, b_edge.reshape(1, hidden), edge_dst, edge_src, w_edge2,
        live, cot, w_node1, b_node.reshape(1, hidden), w_node2,
    )
    probs, keys, grad_moved, active, hidden_grad, grad_t, grad_s, send = call(
        main_kernel, "main", [SMALL] * 3 + [WIDE] * 11,
        (
            ((rows, span), F32), ((granules * span, width), BF16), ((rows, width), BF16),
            ((rows, hidden), BF16), ((rows, hidden), BF16), ((rows, hidden), BF16),
            ((rows, hidden), BF16), ((reps * peers, 32, LANES), BF16),
        ),
        [
            ((rows, span), F32), ((rows, width), BF16), ((rows, width), BF16),
            ((rows, width), BF16), ((rows, hidden), BF16), ((edges, hidden), BF16),
            ((edges, LANES), jnp.int32), ((reps * peers, 32, LANES), F32),
            pltpu.SemaphoreType.DMA((2, rows // 256)), pltpu.SemaphoreType.DMA((3,)),
        ],
        live, partner_first, partner_size, flat, arrived, near, w_node1, lifted,
        w_edge2, cot, flip, edge_dst, slope, edge_src, eager=5,
    )
    part = lax.psum_scatter(send, "rep", scatter_dimension=0, tiled=True)
    back_send, grad_scores = call(
        attend_back_kernel, "attend_back", [SMALL] + [WIDE] * 4,
        (((2 * peers, span, width), BF16), ((rows, span), BF16)),
        [((rows, span), F32)],
        partner_first, grad_moved, keys, probs, flat,
    )
    back_got = exchange(back_send.reshape(slots, block, width), "graph")
    part, back_got = lax.optimization_barrier((part, back_got))
    everything = exchange(
        call(
            share_sum_kernel, "share_sum", [WIDE], (((peers, 32, LANES), BF16),), [],
            exchange(part, "graph"), limit=SMALL_LIMIT,
        ),
        "graph",
    )
    scale = (peers * reps * rows) ** (-0.5)
    share = hidden // reps
    g_edge1, g_bedge, g_edge2, g_node1, g_bnode, g_node2 = call(
        functools.partial(unpack_kernel, scale), "unpack", [WIDE],
        (
            ((2 * width // reps, hidden), F32), ((1, share), F32), ((share, width), F32),
            ((3 * width // reps, hidden), F32), ((1, share), F32), ((share, width), F32),
        ),
        [((peers, 32, LANES), F32)],
        everything, limit=SMALL_LIMIT,
    )
    updated, d_nodes = call(
        finish_kernel, "finish", [SMALL] * 2 + [WIDE] * 13,
        (((rows, width), BF16), ((rows, width), BF16)),
        [((rows, width), F32)],
        live, partner_first, active, hidden_grad, w_node2, w_node1, flat, grad_t, grad_s, w_edge1,
        grad_scores, keys, grad_moved, cot, back_got,
    )
    return (
        updated.reshape(1, granules, block, width),
        d_nodes.reshape(1, granules, block, width),
        g_edge1, g_bedge.reshape(share), g_edge2, g_node1, g_bnode.reshape(share), g_node2,
    )


def solution(mesh):
    placed = (P("rep", "graph", None, None),) * 2 + (P("rep", "graph"),) * 5 + (P(),) * 6
    return jax.shard_map(
        on_device,
        mesh=mesh,
        in_specs=placed,
        out_specs=(
            P("rep", "graph", None, None),
            P("rep", "graph", None, None),
            P("rep", None),
            P("rep"),
            P("rep", None),
            P("rep", None),
            P("rep"),
            P("rep", None),
        ),
        check_vma=False,
    )
```

```python
import functools

import jax
import jax.numpy as jnp
from jax import lax
from jax.experimental import pallas as pl
from jax.experimental.pallas import tpu as pltpu
from jax.sharding import PartitionSpec as P

F32 = jnp.float32
BF16 = jnp.bfloat16
GMAX = 2
LANES = 128
MARK = 16384.0
MARK_LIMIT = 8192.0
VMEM_LIMIT = 63 * 1024 * 1024
SMALL_LIMIT = 16 * 1024 * 1024


def mm(a, b):
    return jnp.dot(a, b, preferred_element_type=F32)


def mm_nt(a, b):
    return lax.dot_general(a, b, (((1,), (1,)), ((), ())), preferred_element_type=F32)


def mm_tn(a, b):
    return lax.dot_general(a, b, (((0,), (0,)), ((), ())), preferred_element_type=F32)


def sigmoid(v):
    return 1.0 / (1.0 + jnp.exp(-v))


def iota(shape, dim):
    return lax.broadcasted_iota(jnp.int32, shape, dim)


def live_rows(live_ref, first, count, block, width):
    limits = [jnp.full((block, width), live_ref[0, first + k], jnp.int32) for k in range(count)]
    positions = iota((block, width), 0)
    return jnp.concatenate([positions] * count, axis=0) < jnp.concatenate(limits, axis=0)


def one_hot(hit):
    return jnp.where(hit, 1.0, 0.0).astype(BF16)


def spread(row_ref):
    return jnp.transpose(jnp.broadcast_to(row_ref[...], (LANES, row_ref.shape[1])))


def flipped(x):
    return jnp.transpose(x.astype(F32)).astype(BF16)


def by_edge(columns, rows):
    lanes = iota(columns.shape, 1)
    return jnp.concatenate(
        [one_hot(columns == lanes + k * LANES) for k in range(rows // LANES)], axis=1
    )


def by_row(row_ref, start, count):
    edges = row_ref.shape[1]
    return one_hot(
        jnp.broadcast_to(row_ref[...], (count, edges)) == iota((count, edges), 0) + start
    )


def pack_kernel(live_ref, first_ref, nodes_ref, out_ref, marked_ref, sems):
    granules, block, width = nodes_ref.shape
    rows, columns = iota((block, width), 0), iota((block, width), 1)
    copies = []
    for g in range(granules):
        slot = (first_ref[0, g] // granules) * (2 * GMAX) + (GMAX if g < granules // 2 else 0)
        if g > 0:
            slot = slot + (first_ref[0, g] == first_ref[0, g - 1]).astype(jnp.int32)
        marked = (rows >= live_ref[0, g]) & (columns == 0)
        marked_ref[g] = jnp.where(marked, MARK, nodes_ref[g].astype(F32)).astype(BF16)
        copy = pltpu.make_async_copy(marked_ref.at[g], out_ref.at[slot], sems.at[g])
        copy.start()
        copies.append(copy)
    for copy in copies:
        copy.wait()


def edge_forward_kernel(
    nodes_ref, w1_ref, b_ref, dst_ref, src_ref, w2_ref, live_ref, cot_ref, wn1_ref, bn_ref, wn2_ref,
    flip_ref, slope_ref, near_ref, lifted_ref,
    pre_t, pre_s, terms, col_t, col_s,
):
    rows, width = nodes_ref.shape
    edges = src_ref.shape[1]
    chunk = 256
    granules = live_ref.shape[1]
    block = rows // granules
    for k in range(rows // chunk):
        at = pl.ds(k * chunk, chunk)
        x = nodes_ref[at, :]
        pre_t[at, :] = (mm(x, w1_ref[:width, :]) + b_ref[...]).astype(BF16)
        pre_s[at, :] = mm(x, w1_ref[width:, :]).astype(BF16)
    col_t[...] = spread(dst_ref)
    col_s[...] = spread(src_ref)
    for k in range(edges // chunk):
        at = pl.ds(k * chunk, chunk)
        summed = mm(by_edge(col_t[at, :], rows), pre_t[...]) + mm(
            by_edge(col_s[at, :], rows), pre_s[...]
        )
        s = sigmoid(summed)
        terms[at, :] = (summed * s).astype(BF16)
        slope_ref[at, :] = (s * (1.0 + summed * (1.0 - s))).astype(BF16)
    for k in range(rows // chunk):
        at = pl.ds(k * chunk, chunk)
        gathered = mm(by_row(dst_ref, k * chunk, chunk), terms[...]).astype(BF16)
        message = mm(gathered, w2_ref[...]).astype(BF16)
        flip_ref[pl.ds(0, width), at] = flipped(nodes_ref[at, :])
        flip_ref[pl.ds(width, width), at] = flipped(message)
        flip_ref[pl.ds(2 * width, gathered.shape[1]), at] = flipped(gathered)
        near_ref[at, :] = (
            mm(nodes_ref[at, :], wn1_ref[:width, :])
            + mm(message, wn1_ref[width : 2 * width, :])
            + bn_ref[...]
        )
        mask = live_rows(live_ref, k * (chunk // block), chunk // block, block, width)
        go = jnp.where(mask, cot_ref[at, :].astype(F32), 0.0).astype(BF16)
        lifted_ref[at, :] = mm_nt(go, wn2_ref[...])


def deal(stage, value, first_row, per_rep, base):
    rows, width = value.shape
    across = width // LANES
    for i in range(rows // 8):
        rep, inner = divmod(first_row + 8 * i, per_rep)
        for c in range(across):
            unit = base + (inner // 8) * across + c
            at = rep * 32 + unit % 32
            stage[at, pl.ds(unit // 32 * 8, 8), :] = value[
                8 * i : 8 * i + 8, c * LANES : (c + 1) * LANES
            ]


def main_kernel(
    live_ref, first_ref, size_ref, nodes_ref, arrived_ref, near_ref, wn1_ref, lifted_ref,
    w2_ref, cot_ref, flip_ref, dst_ref, slope_ref, src_ref,
    probs_ref, keys_ref, gmov_ref, active, hidden_grad, grad_t, grad_s, send_ref,
    scores, moved, out_grad, gmsg, wide_grad, terms, col_t, stage, row_sems, send_sems,
):
    rows, width = nodes_ref.shape
    granules = live_ref.shape[1]
    block = rows // granules
    span = GMAX * block
    scale = width ** (-0.5)
    pick = jnp.where((iota((16, width), 0) == 0) & (iota((16, width), 1) == 0), 1.0, 0.0).astype(BF16)
    span_rows = iota((span, width), 0)
    span_lanes = iota((1, span), 1)
    arrived_ref.wait()
    for later in (near_ref, wn1_ref, lifted_ref, w2_ref, cot_ref):
        later.start()
    for g in range(granules):
        pair = (first_ref[0, g] // granules) * 2 + (0 if g < granules // 2 else 1)
        filled = size_ref[0, g] * block
        raw = arrived_ref[pair]
        wide = raw.astype(F32)
        valid = (jnp.broadcast_to(wide[:, 0:1], wide.shape) < MARK_LIMIT) & (span_rows < filled)
        keys_ref[pl.ds(g * span, span), :] = jnp.where(valid, wide, 0.0).astype(BF16)
        q = nodes_ref[pl.ds(g * block, block), :]
        s = mm_nt(jnp.concatenate([q, pick], axis=0), raw)
        live_key = (s[block : block + 1, :] < MARK_LIMIT) & (span_lanes < filled)
        scores[pl.ds(g * block, block), :] = jnp.where(live_key, s[:block, :] * scale, -1e30)
    keys_ref.flush()
    for later in (flip_ref, dst_ref, slope_ref, src_ref):
        later.start()
    s = scores[...]
    powers = jnp.exp(s - jnp.max(s, axis=-1, keepdims=True))
    probs_ref[...] = powers / jnp.sum(powers, axis=-1, keepdims=True)
    probs_ref.flush()
    for g in range(granules):
        at = pl.ds(g * block, block)
        context = mm(probs_ref[at, :].astype(BF16), keys_ref[pl.ds(g * span, span), :])
        moved[at, :] = (nodes_ref[at, :].astype(F32) - context).astype(BF16)

    chunk = 512
    per = chunk // block
    for k in range(rows // chunk):
        at = pl.ds(k * chunk, chunk)
        hidden = near_ref[at, :] + mm(moved[at, :], wn1_ref[2 * width :, :])
        s = sigmoid(hidden)
        act = (hidden * s).astype(BF16)
        active[at, :] = act
        gh = (lifted_ref[at, :] * (s * (1.0 + hidden * (1.0 - s)))).astype(BF16)
        hidden_grad[at, :] = gh
        gm = mm_nt(gh, wn1_ref[width : 2 * width, :]).astype(BF16)
        gmsg[at, :] = gm
        gmov_ref[at, :] = mm_nt(gh, wn1_ref[2 * width :, :]).astype(BF16)
        wide_grad[at, :] = mm_nt(gm, w2_ref[...]).astype(BF16)
        mask = live_rows(live_ref, k * per, per, block, width)
        out_grad[at, :] = jnp.where(mask, cot_ref[at, :].astype(F32), 0.0).astype(BF16)
    gmov_ref.flush()
    active.flush()
    hidden_grad.flush()
    gh = hidden_grad[...]
    node_bias = jnp.sum(gh.astype(F32), axis=0, keepdims=True)
    deal(stage, mm(flip_ref[pl.ds(0, 2 * width), :], gh), 0, 96, 0)
    deal(stage, mm_tn(moved[...], gh), 2 * width, 96, 0)
    deal(stage, mm_tn(active[...], out_grad[...]), 0, 64, 48)

    edges = src_ref.shape[1]
    col_t[...] = spread(dst_ref)
    for k in range(edges // chunk):
        at = pl.ds(k * chunk, chunk)
        terms[at, :] = (
            mm(by_edge(col_t[at, :], rows), wide_grad[...]) * slope_ref[at, :].astype(F32)
        ).astype(BF16)
    deal(stage, mm(flip_ref[pl.ds(2 * width, gh.shape[1]), :], gmsg[...]), 0, 64, 96)
    cuts = [(pl.ds(0, 256), pl.ds(0, 16)), (pl.ds(0, 128), pl.ds(16, 16)), (pl.ds(128, 128), pl.ds(16, 16))]
    sends = send_ref.pieces(cuts, send_sems)
    send_ref[:, pl.ds(0, 16), :] = stage[:, pl.ds(0, 16), :].astype(BF16)
    sends[0].start()
    row_cuts = [(pl.ds(k * chunk, chunk),) for k in range(rows // chunk)]
    rows_t = grad_t.pieces(row_cuts, row_sems.at[0])
    rows_s = grad_s.pieces(row_cuts, row_sems.at[1])
    edge_bias = jnp.zeros((1, terms.shape[1]), F32)
    for k in range(rows // chunk):
        at = pl.ds(k * chunk, chunk)
        gt = mm(by_row(dst_ref, k * chunk, chunk), terms[...]).astype(BF16)
        gs = mm(by_row(src_ref, k * chunk, chunk), terms[...]).astype(BF16)
        grad_t[at, :] = gt
        grad_s[at, :] = gs
        edge_bias = edge_bias + jnp.sum(gt.astype(F32), axis=0, keepdims=True)
        rows_t[k].start()
        rows_s[k].start()
    biases = jnp.concatenate(
        [edge_bias, node_bias, jnp.zeros((6, edge_bias.shape[1]), F32)], axis=0
    )
    for rep in range(8):
        piece = biases[:, rep // 2 * LANES : (rep // 2 + 1) * LANES]
        for share in range(16, 32):
            stage[rep * 32 + share, pl.ds(24, 8), :] = piece
    x = flip_ref[pl.ds(0, width), :]
    for half, grad in enumerate((grad_t, grad_s)):
        deal(stage, mm(x, grad[...]), half * width, 64, 64)
        at = pl.ds(half * 128, 128)
        send_ref[at, pl.ds(16, 16), :] = stage[at, pl.ds(16, 16), :].astype(BF16)
        sends[1 + half].start()


def attend_back_kernel(
    first_ref, gmov_ref, keys_ref, probs_ref, nodes_ref,
    back_ref, gscores_ref,
    prob_grad,
):
    rows, width = nodes_ref.shape
    granules = first_ref.shape[1]
    block = rows // granules
    span = GMAX * block
    scale = width ** (-0.5)
    for g in range(granules):
        at = pl.ds(g * block, block)
        prob_grad[at, :] = -mm_nt(gmov_ref[at, :], keys_ref[pl.ds(g * span, span), :])
    probs = probs_ref[...]
    inner = jnp.sum(probs * prob_grad[...], axis=-1, keepdims=True)
    gscores_ref[...] = (probs * (prob_grad[...] - inner) * scale).astype(BF16)
    gscores_ref.flush()
    held = None
    for g in range(granules):
        at = pl.ds(g * block, block)
        pair = (first_ref[0, g] // granules) * 2 + (0 if g < granules // 2 else 1)
        left = jnp.concatenate([probs_ref[at, :].astype(BF16), gscores_ref[at, :]], axis=0)
        right = jnp.concatenate([-gmov_ref[at, :], nodes_ref[at, :]], axis=0)
        new = mm_tn(left, right)
        if held is None:
            held = new
        else:
            held = new + jnp.where(first_ref[0, g] == first_ref[0, g - 1], held, 0.0)
        back_ref[pair] = held.astype(BF16)


def finish_kernel(
    live_ref, first_ref, active, hidden_grad, wn2_ref, wn1_ref, nodes_ref, grad_t, grad_s, w1_ref,
    gscores_ref, keys_ref, gmov_ref, cot_ref, back_ref,
    updated_ref, out_ref,
    base,
):
    rows, width = nodes_ref.shape
    granules = live_ref.shape[1]
    block = rows // granules
    span = GMAX * block
    chunk = 256
    per = chunk // block
    for k in range(rows // chunk):
        at = pl.ds(k * chunk, chunk)
        mask = live_rows(live_ref, k * per, per, block, width)
        updated_ref[at, :] = jnp.where(
            mask, nodes_ref[at, :].astype(F32) + mm(active[at, :], wn2_ref[...]), 0.0
        ).astype(BF16)
        base[at, :] = (
            mm_nt(hidden_grad[at, :], wn1_ref[:width, :])
            + mm_nt(grad_t[at, :], w1_ref[:width, :])
            + mm_nt(grad_s[at, :], w1_ref[width:, :])
        )
    updated_ref.flush()
    positions = iota((block, width), 0)
    for g in range(granules):
        at = pl.ds(g * block, block)
        slot = (first_ref[0, g] // granules) * (2 * GMAX) + (GMAX if g < granules // 2 else 0)
        if g > 0:
            slot = slot + (first_ref[0, g] == first_ref[0, g - 1]).astype(jnp.int32)
        total = (
            base[at, :]
            + cot_ref[at, :].astype(F32)
            + gmov_ref[at, :].astype(F32)
            + mm(gscores_ref[at, :], keys_ref[pl.ds(g * span, span), :])
            + back_ref[slot].astype(F32)
        )
        out_ref[at, :] = jnp.where(positions < live_ref[0, g], total, 0.0).astype(BF16)


def share_sum_kernel(got_ref, out_ref):
    total = got_ref[0].astype(F32)
    for k in range(1, got_ref.shape[0]):
        total = total + got_ref[k].astype(F32)
    low = total.astype(BF16)
    for k in range(out_ref.shape[0]):
        out_ref[k] = low


def collect(out_ref, wide, base, scale):
    rows, width = out_ref.shape
    across = width // LANES
    for i in range(rows // 8):
        for c in range(across):
            unit = base + i * across + c
            out_ref[pl.ds(8 * i, 8), pl.ds(c * LANES, LANES)] = (
                wide[unit % 32, pl.ds(unit // 32 * 8, 8), :] * scale
            )


def unpack_kernel(scale, all_ref, e1_ref, be_ref, e2_ref, n1_ref, bn_ref, n2_ref, wide):
    wide[...] = all_ref[...].astype(F32)
    collect(n1_ref, wide, 0, scale)
    collect(n2_ref, wide, 48, scale)
    collect(e1_ref, wide, 64, scale)
    collect(e2_ref, wide, 96, scale)
    biases = wide[16, pl.ds(24, 8), :] * scale
    half = LANES // 2
    piece = jnp.where(lax.rem(lax.axis_index("rep"), 2) == 0, biases[:, :half], biases[:, half:])
    be_ref[...] = piece[0:1, :]
    bn_ref[...] = piece[1:2, :]


class Fetched:
    def __init__(self, ref, copy):
        self.ref, self.copy, self.shape = ref, copy, ref.shape
        self.started = self.ready = False

    def start(self):
        if not self.started:
            self.copy.start()
            self.started = True

    def wait(self):
        self.start()
        if not self.ready:
            self.copy.wait()
            self.ready = True
        return self.ref

    def __getitem__(self, at):
        return self.wait()[at]


class Written:
    def __init__(self, ref, out, copy):
        self.ref, self.out, self.copy, self.shape, self.sent = ref, out, copy, ref.shape, False

    def __setitem__(self, at, value):
        self.ref[at] = value

    def __getitem__(self, at):
        return self.ref[at]

    def flush(self):
        self.copy.start()
        self.sent = True

    def pieces(self, cuts, sems):
        self.sent = True
        self.copy = Many(
            [pltpu.make_async_copy(self.ref.at[c], self.out.at[c], sems.at[k]) for k, c in enumerate(cuts)]
        )
        return self.copy.copies


class Many:
    def __init__(self, copies):
        self.copies = copies

    def wait(self):
        for copy in self.copies:
            copy.wait()


HB = pl.BlockSpec(memory_space=pltpu.HBM)
SMALL, WIDE, RAW = 0, 1, 2


def call(kernel, name, kinds, outs, scratch, *args, raw_out=False, limit=VMEM_LIMIT, eager=99):
    fetched = [k for k, kind in enumerate(kinds) if kind != RAW]
    n_in, n_out = len(args), len(outs)

    def body(*refs):
        ins, results = refs[:n_in], refs[n_in : n_in + n_out]
        rest = list(refs[n_in + n_out :])
        in_sem, out_sem = rest.pop(0), rest.pop(0)
        given = list(ins)
        for at, k in enumerate(fetched):
            copy = pltpu.make_async_copy(ins[k], rest[at], in_sem.at[at])
            given[k] = Fetched(rest[at], copy)
            if k < eager:
                given[k].start()
        rest = rest[len(fetched) :]
        if raw_out:
            written = list(results)
        else:
            written = [
                Written(
                    rest[k], results[k], pltpu.make_async_copy(rest[k], results[k], out_sem.at[k])
                )
                for k in range(n_out)
            ]
            rest = rest[n_out:]
        kernel(*given, *written, *rest)
        for one in given:
            if isinstance(one, Fetched):
                one.wait()
        if not raw_out:
            for one in written:
                if not one.sent:
                    one.flush()
            for one in written:
                one.copy.wait()

    buffers = [
        (pltpu.SMEM if kinds[k] == SMALL else pltpu.VMEM)(args[k].shape, args[k].dtype)
        for k in fetched
    ]
    if not raw_out:
        buffers += [pltpu.VMEM(s, d) for s, d in outs]
    got = pl.pallas_call(
        body,
        name=name,
        out_shape=tuple(jax.ShapeDtypeStruct(s, d) for s, d in outs),
        in_specs=[HB] * n_in,
        out_specs=(HB,) * n_out,
        scratch_shapes=[
            pltpu.SemaphoreType.DMA((max(len(fetched), 1),)),
            pltpu.SemaphoreType.DMA((n_out,)),
            *buffers,
            *[s if not isinstance(s, tuple) else pltpu.VMEM(*s) for s in scratch],
        ],
        compiler_params=pltpu.CompilerParams(vmem_limit_bytes=limit),
    )(*args)
    return got[0] if n_out == 1 else got


def exchange(x, axis):
    return lax.all_to_all(x, axis, split_axis=0, concat_axis=0, tiled=True)


def on_device(
    nodes, cotangent, live, partner_first, partner_size, edge_src, edge_dst,
    w_edge1, b_edge, w_edge2, w_node1, b_node, w_node2,
):
    granules, block, width = nodes.shape[1:]
    rows = granules * block
    edges = edge_src.shape[1]
    hidden = w_edge1.shape[1]
    peers, reps = lax.axis_size("graph"), lax.axis_size("rep")
    blocks = nodes[0]
    flat = blocks.reshape(rows, width)
    cot = cotangent[0].reshape(rows, width)
    slots = peers * 2 * GMAX
    span = GMAX * block

    outgoing = call(
        pack_kernel, "pack", [SMALL, SMALL, WIDE], (((slots, block, width), BF16),),
        [((granules, block, width), BF16), pltpu.SemaphoreType.DMA((granules,))],
        live, partner_first, blocks, raw_out=True,
    )
    arrived = exchange(outgoing, "graph").reshape(2 * peers, span, width)
    flip, slope, near, lifted = call(
        edge_forward_kernel, "edge_forward", [WIDE] * 6 + [SMALL] + [WIDE] * 4,
        (
            ((2 * width + hidden, rows), BF16), ((edges, hidden), BF16),
            ((rows, hidden), F32), ((rows, hidden), F32),
        ),
        [
            ((rows, hidden), BF16), ((rows, hidden), BF16), ((edges, hidden), BF16),
            ((edges, LANES), jnp.int32), ((edges, LANES), jnp.int32),
        ],
        flat, w_edge1, b_edge.reshape(1, hidden), edge_dst, edge_src, w_edge2,
        live, cot, w_node1, b_node.reshape(1, hidden), w_node2,
    )
    probs, keys, grad_moved, active, hidden_grad, grad_t, grad_s, send = call(
        main_kernel, "main", [SMALL] * 3 + [WIDE] * 11,
        (
            ((rows, span), F32), ((granules * span, width), BF16), ((rows, width), BF16),
            ((rows, hidden), BF16), ((rows, hidden), BF16), ((rows, hidden), BF16),
            ((rows, hidden), BF16), ((reps * peers, 32, LANES), BF16),
        ),
        [
            ((rows, span), F32), ((rows, width), BF16), ((rows, width), BF16),
            ((rows, width), BF16), ((rows, hidden), BF16), ((edges, hidden), BF16),
            ((edges, LANES), jnp.int32), ((reps * peers, 32, LANES), F32),
            pltpu.SemaphoreType.DMA((2, rows // 512)), pltpu.SemaphoreType.DMA((3,)),
        ],
        live, partner_first, partner_size, flat, arrived, near, w_node1, lifted,
        w_edge2, cot, flip, edge_dst, slope, edge_src, eager=5,
    )
    part = lax.psum_scatter(send, "rep", scatter_dimension=0, tiled=True)
    back_send, grad_scores = call(
        attend_back_kernel, "attend_back", [SMALL] + [WIDE] * 4,
        (((2 * peers, span, width), BF16), ((rows, span), BF16)),
        [((rows, span), F32)],
        partner_first, grad_moved, keys, probs, flat,
    )
    back_got = exchange(back_send.reshape(slots, block, width), "graph")
    part, back_got = lax.optimization_barrier((part, back_got))
    everything = exchange(
        call(
            share_sum_kernel, "share_sum", [WIDE], (((peers, 32, LANES), BF16),), [],
            exchange(part, "graph"), limit=SMALL_LIMIT,
        ),
        "graph",
    )
    scale = (peers * reps * rows) ** (-0.5)
    share = hidden // reps
    g_edge1, g_bedge, g_edge2, g_node1, g_bnode, g_node2 = call(
        functools.partial(unpack_kernel, scale), "unpack", [WIDE],
        (
            ((2 * width // reps, hidden), F32), ((1, share), F32), ((share, width), F32),
            ((3 * width // reps, hidden), F32), ((1, share), F32), ((share, width), F32),
        ),
        [((peers, 32, LANES), F32)],
        everything, limit=SMALL_LIMIT,
    )
    updated, d_nodes = call(
        finish_kernel, "finish", [SMALL] * 2 + [WIDE] * 13,
        (((rows, width), BF16), ((rows, width), BF16)),
        [((rows, width), F32)],
        live, partner_first, active, hidden_grad, w_node2, w_node1, flat, grad_t, grad_s, w_edge1,
        grad_scores, keys, grad_moved, cot, back_got,
    )
    return (
        updated.reshape(1, granules, block, width),
        d_nodes.reshape(1, granules, block, width),
        g_edge1, g_bedge.reshape(share), g_edge2, g_node1, g_bnode.reshape(share), g_node2,
    )


def solution(mesh):
    placed = (P("rep", "graph", None, None),) * 2 + (P("rep", "graph"),) * 5 + (P(),) * 6
    return jax.shard_map(
        on_device,
        mesh=mesh,
        in_specs=placed,
        out_specs=(
            P("rep", "graph", None, None),
            P("rep", "graph", None, None),
            P("rep", None),
            P("rep"),
            P("rep", None),
            P("rep", None),
            P("rep"),
            P("rep", None),
        ),
        check_vma=False,
    )
```

```python
import functools

import jax
import jax.numpy as jnp
from jax import lax
from jax.experimental import pallas as pl
from jax.experimental.pallas import tpu as pltpu
from jax.sharding import PartitionSpec as P

F32 = jnp.float32
BF16 = jnp.bfloat16
GMAX = 2
LANES = 128
MARK = 16384.0
MARK_LIMIT = 8192.0
VMEM_LIMIT = 63 * 1024 * 1024
SMALL_LIMIT = 16 * 1024 * 1024


def mm(a, b):
    return jnp.dot(a, b, preferred_element_type=F32)


def mm_nt(a, b):
    return lax.dot_general(a, b, (((1,), (1,)), ((), ())), preferred_element_type=F32)


def mm_tn(a, b):
    return lax.dot_general(a, b, (((0,), (0,)), ((), ())), preferred_element_type=F32)


def sigmoid(v):
    return 1.0 / (1.0 + jnp.exp(-v))


def iota(shape, dim):
    return lax.broadcasted_iota(jnp.int32, shape, dim)


def live_rows(live_ref, first, count, block, width):
    limits = [jnp.full((block, width), live_ref[0, first + k], jnp.int32) for k in range(count)]
    positions = iota((block, width), 0)
    return jnp.concatenate([positions] * count, axis=0) < jnp.concatenate(limits, axis=0)


def one_hot(hit):
    return jnp.where(hit, 1.0, 0.0).astype(BF16)


def spread(row_ref):
    return jnp.transpose(jnp.broadcast_to(row_ref[...], (LANES, row_ref.shape[1])))


def flipped(x):
    return jnp.transpose(x.astype(F32)).astype(BF16)


def by_edge(columns, rows):
    lanes = iota(columns.shape, 1)
    return jnp.concatenate(
        [one_hot(columns == lanes + k * LANES) for k in range(rows // LANES)], axis=1
    )


def by_row(row_ref, start, count):
    edges = row_ref.shape[1]
    return one_hot(
        jnp.broadcast_to(row_ref[...], (count, edges)) == iota((count, edges), 0) + start
    )


def pack_kernel(live_ref, first_ref, nodes_ref, out_ref, marked_ref, sems):
    granules, block, width = nodes_ref.shape
    rows, columns = iota((block, width), 0), iota((block, width), 1)
    copies = []
    for g in range(granules):
        slot = (first_ref[0, g] // granules) * (2 * GMAX) + (GMAX if g < granules // 2 else 0)
        if g > 0:
            slot = slot + (first_ref[0, g] == first_ref[0, g - 1]).astype(jnp.int32)
        marked = (rows >= live_ref[0, g]) & (columns == 0)
        marked_ref[g] = jnp.where(marked, MARK, nodes_ref[g].astype(F32)).astype(BF16)
        copy = pltpu.make_async_copy(marked_ref.at[g], out_ref.at[slot], sems.at[g])
        copy.start()
        copies.append(copy)
    for copy in copies:
        copy.wait()


def edge_forward_kernel(
    nodes_ref, w1_ref, b_ref, dst_ref, src_ref, w2_ref, live_ref, cot_ref, wn1_ref, bn_ref, wn2_ref,
    flip_ref, slope_ref, near_ref, lifted_ref,
    pre_t, pre_s, terms, col_t, col_s,
):
    rows, width = nodes_ref.shape
    edges = src_ref.shape[1]
    chunk = 256
    granules = live_ref.shape[1]
    block = rows // granules
    for k in range(rows // chunk):
        at = pl.ds(k * chunk, chunk)
        x = nodes_ref[at, :]
        pre_t[at, :] = (mm(x, w1_ref[:width, :]) + b_ref[...]).astype(BF16)
        pre_s[at, :] = mm(x, w1_ref[width:, :]).astype(BF16)
    col_t[...] = spread(dst_ref)
    col_s[...] = spread(src_ref)
    for k in range(edges // chunk):
        at = pl.ds(k * chunk, chunk)
        summed = mm(by_edge(col_t[at, :], rows), pre_t[...]) + mm(
            by_edge(col_s[at, :], rows), pre_s[...]
        )
        s = sigmoid(summed)
        terms[at, :] = (summed * s).astype(BF16)
        slope_ref[at, :] = (s * (1.0 + summed * (1.0 - s))).astype(BF16)
    for k in range(rows // chunk):
        at = pl.ds(k * chunk, chunk)
        gathered = mm(by_row(dst_ref, k * chunk, chunk), terms[...]).astype(BF16)
        message = mm(gathered, w2_ref[...]).astype(BF16)
        flip_ref[pl.ds(0, width), at] = flipped(nodes_ref[at, :])
        flip_ref[pl.ds(width, width), at] = flipped(message)
        flip_ref[pl.ds(2 * width, gathered.shape[1]), at] = flipped(gathered)
        near_ref[at, :] = (
            mm(nodes_ref[at, :], wn1_ref[:width, :])
            + mm(message, wn1_ref[width : 2 * width, :])
            + bn_ref[...]
        )
        mask = live_rows(live_ref, k * (chunk // block), chunk // block, block, width)
        go = jnp.where(mask, cot_ref[at, :].astype(F32), 0.0).astype(BF16)
        lifted_ref[at, :] = mm_nt(go, wn2_ref[...])


def deal(stage, value, first_row, per_rep, base):
    rows, width = value.shape
    across = width // LANES
    for i in range(rows // 8):
        rep, inner = divmod(first_row + 8 * i, per_rep)
        for c in range(across):
            unit = base + (inner // 8) * across + c
            at = rep * 32 + unit % 32
            stage[at, pl.ds(unit // 32 * 8, 8), :] = value[
                8 * i : 8 * i + 8, c * LANES : (c + 1) * LANES
            ]


def main_kernel(
    live_ref, first_ref, size_ref, nodes_ref, arrived_ref, near_ref, wn1_ref, lifted_ref,
    w2_ref, cot_ref, flip_ref, dst_ref, slope_ref, src_ref,
    probs_ref, keys_ref, gmov_ref, active, hidden_grad, grad_t, grad_s, send_ref,
    scores, moved, out_grad, gmsg, wide_grad, terms, col_t, stage, row_sems, send_sems,
):
    rows, width = nodes_ref.shape
    granules = live_ref.shape[1]
    block = rows // granules
    span = GMAX * block
    scale = width ** (-0.5)
    pick = jnp.where((iota((16, width), 0) == 0) & (iota((16, width), 1) == 0), 1.0, 0.0).astype(BF16)
    span_rows = iota((span, width), 0)
    span_lanes = iota((1, span), 1)
    arrived_ref.wait()
    for later in (near_ref, wn1_ref, lifted_ref, w2_ref, cot_ref):
        later.start()
    for g in range(granules):
        pair = (first_ref[0, g] // granules) * 2 + (0 if g < granules // 2 else 1)
        filled = size_ref[0, g] * block
        raw = arrived_ref[pair]
        wide = raw.astype(F32)
        valid = (jnp.broadcast_to(wide[:, 0:1], wide.shape) < MARK_LIMIT) & (span_rows < filled)
        keys_ref[pl.ds(g * span, span), :] = jnp.where(valid, wide, 0.0).astype(BF16)
        q = nodes_ref[pl.ds(g * block, block), :]
        s = mm_nt(jnp.concatenate([q, pick], axis=0), raw)
        live_key = (s[block : block + 1, :] < MARK_LIMIT) & (span_lanes < filled)
        scores[pl.ds(g * block, block), :] = jnp.where(live_key, s[:block, :] * scale, -1e30)
    keys_ref.flush()
    for later in (flip_ref, dst_ref, slope_ref, src_ref):
        later.start()
    s = scores[...]
    powers = jnp.exp(s - jnp.max(s, axis=-1, keepdims=True))
    probs_ref[...] = powers / jnp.sum(powers, axis=-1, keepdims=True)
    probs_ref.flush()
    for g in range(granules):
        at = pl.ds(g * block, block)
        context = mm(probs_ref[at, :].astype(BF16), keys_ref[pl.ds(g * span, span), :])
        moved[at, :] = (nodes_ref[at, :].astype(F32) - context).astype(BF16)

    chunk = 1024
    per = chunk // block
    for k in range(rows // chunk):
        at = pl.ds(k * chunk, chunk)
        hidden = near_ref[at, :] + mm(moved[at, :], wn1_ref[2 * width :, :])
        s = sigmoid(hidden)
        act = (hidden * s).astype(BF16)
        active[at, :] = act
        gh = (lifted_ref[at, :] * (s * (1.0 + hidden * (1.0 - s)))).astype(BF16)
        hidden_grad[at, :] = gh
        gm = mm_nt(gh, wn1_ref[width : 2 * width, :]).astype(BF16)
        gmsg[at, :] = gm
        gmov_ref[at, :] = mm_nt(gh, wn1_ref[2 * width :, :]).astype(BF16)
        wide_grad[at, :] = mm_nt(gm, w2_ref[...]).astype(BF16)
        mask = live_rows(live_ref, k * per, per, block, width)
        out_grad[at, :] = jnp.where(mask, cot_ref[at, :].astype(F32), 0.0).astype(BF16)
    gmov_ref.flush()
    active.flush()
    hidden_grad.flush()
    gh = hidden_grad[...]
    node_bias = jnp.sum(gh.astype(F32), axis=0, keepdims=True)
    deal(stage, mm(flip_ref[pl.ds(0, 2 * width), :], gh), 0, 96, 0)
    deal(stage, mm_tn(moved[...], gh), 2 * width, 96, 0)
    deal(stage, mm_tn(active[...], out_grad[...]), 0, 64, 48)

    edges = src_ref.shape[1]
    col_t[...] = spread(dst_ref)
    for k in range(edges // chunk):
        at = pl.ds(k * chunk, chunk)
        terms[at, :] = (
            mm(by_edge(col_t[at, :], rows), wide_grad[...]) * slope_ref[at, :].astype(F32)
        ).astype(BF16)
    deal(stage, mm(flip_ref[pl.ds(2 * width, gh.shape[1]), :], gmsg[...]), 0, 64, 96)
    cuts = [(pl.ds(0, 256), pl.ds(0, 16)), (pl.ds(0, 128), pl.ds(16, 16)), (pl.ds(128, 128), pl.ds(16, 16))]
    sends = send_ref.pieces(cuts, send_sems)
    send_ref[:, pl.ds(0, 16), :] = stage[:, pl.ds(0, 16), :].astype(BF16)
    sends[0].start()
    row_cuts = [(pl.ds(k * chunk, chunk),) for k in range(rows // chunk)]
    rows_t = grad_t.pieces(row_cuts, row_sems.at[0])
    rows_s = grad_s.pieces(row_cuts, row_sems.at[1])
    edge_bias = jnp.zeros((1, terms.shape[1]), F32)
    for k in range(rows // chunk):
        at = pl.ds(k * chunk, chunk)
        gt = mm(by_row(dst_ref, k * chunk, chunk), terms[...]).astype(BF16)
        gs = mm(by_row(src_ref, k * chunk, chunk), terms[...]).astype(BF16)
        grad_t[at, :] = gt
        grad_s[at, :] = gs
        edge_bias = edge_bias + jnp.sum(gt.astype(F32), axis=0, keepdims=True)
        rows_t[k].start()
        rows_s[k].start()
    biases = jnp.concatenate(
        [edge_bias, node_bias, jnp.zeros((6, edge_bias.shape[1]), F32)], axis=0
    )
    for rep in range(8):
        piece = biases[:, rep // 2 * LANES : (rep // 2 + 1) * LANES]
        for share in range(16, 32):
            stage[rep * 32 + share, pl.ds(24, 8), :] = piece
    x = flip_ref[pl.ds(0, width), :]
    for half, grad in enumerate((grad_t, grad_s)):
        deal(stage, mm(x, grad[...]), half * width, 64, 64)
        at = pl.ds(half * 128, 128)
        send_ref[at, pl.ds(16, 16), :] = stage[at, pl.ds(16, 16), :].astype(BF16)
        sends[1 + half].start()


def attend_back_kernel(
    first_ref, gmov_ref, keys_ref, probs_ref, nodes_ref,
    back_ref, gscores_ref,
    prob_grad,
):
    rows, width = nodes_ref.shape
    granules = first_ref.shape[1]
    block = rows // granules
    span = GMAX * block
    scale = width ** (-0.5)
    for g in range(granules):
        at = pl.ds(g * block, block)
        prob_grad[at, :] = -mm_nt(gmov_ref[at, :], keys_ref[pl.ds(g * span, span), :])
    probs = probs_ref[...]
    inner = jnp.sum(probs * prob_grad[...], axis=-1, keepdims=True)
    gscores_ref[...] = (probs * (prob_grad[...] - inner) * scale).astype(BF16)
    gscores_ref.flush()
    held = None
    for g in range(granules):
        at = pl.ds(g * block, block)
        pair = (first_ref[0, g] // granules) * 2 + (0 if g < granules // 2 else 1)
        left = jnp.concatenate([probs_ref[at, :].astype(BF16), gscores_ref[at, :]], axis=0)
        right = jnp.concatenate([-gmov_ref[at, :], nodes_ref[at, :]], axis=0)
        new = mm_tn(left, right)
        if held is None:
            held = new
        else:
            held = new + jnp.where(first_ref[0, g] == first_ref[0, g - 1], held, 0.0)
        back_ref[pair] = held.astype(BF16)


def finish_kernel(
    live_ref, first_ref, active, hidden_grad, wn2_ref, wn1_ref, nodes_ref, grad_t, grad_s, w1_ref,
    gscores_ref, keys_ref, gmov_ref, cot_ref, back_ref,
    updated_ref, out_ref,
    base,
):
    rows, width = nodes_ref.shape
    granules = live_ref.shape[1]
    block = rows // granules
    span = GMAX * block
    chunk = 256
    per = chunk // block
    for k in range(rows // chunk):
        at = pl.ds(k * chunk, chunk)
        mask = live_rows(live_ref, k * per, per, block, width)
        updated_ref[at, :] = jnp.where(
            mask, nodes_ref[at, :].astype(F32) + mm(active[at, :], wn2_ref[...]), 0.0
        ).astype(BF16)
        base[at, :] = (
            mm_nt(hidden_grad[at, :], wn1_ref[:width, :])
            + mm_nt(grad_t[at, :], w1_ref[:width, :])
            + mm_nt(grad_s[at, :], w1_ref[width:, :])
        )
    updated_ref.flush()
    positions = iota((block, width), 0)
    for g in range(granules):
        at = pl.ds(g * block, block)
        slot = (first_ref[0, g] // granules) * (2 * GMAX) + (GMAX if g < granules // 2 else 0)
        if g > 0:
            slot = slot + (first_ref[0, g] == first_ref[0, g - 1]).astype(jnp.int32)
        total = (
            base[at, :]
            + cot_ref[at, :].astype(F32)
            + gmov_ref[at, :].astype(F32)
            + mm(gscores_ref[at, :], keys_ref[pl.ds(g * span, span), :])
            + back_ref[slot].astype(F32)
        )
        out_ref[at, :] = jnp.where(positions < live_ref[0, g], total, 0.0).astype(BF16)


def share_sum_kernel(got_ref, out_ref):
    total = got_ref[0].astype(F32)
    for k in range(1, got_ref.shape[0]):
        total = total + got_ref[k].astype(F32)
    low = total.astype(BF16)
    for k in range(out_ref.shape[0]):
        out_ref[k] = low


def collect(out_ref, wide, base, scale):
    rows, width = out_ref.shape
    across = width // LANES
    for i in range(rows // 8):
        for c in range(across):
            unit = base + i * across + c
            out_ref[pl.ds(8 * i, 8), pl.ds(c * LANES, LANES)] = (
                wide[unit % 32, pl.ds(unit // 32 * 8, 8), :] * scale
            )


def unpack_kernel(scale, all_ref, e1_ref, be_ref, e2_ref, n1_ref, bn_ref, n2_ref, wide):
    wide[...] = all_ref[...].astype(F32)
    collect(n1_ref, wide, 0, scale)
    collect(n2_ref, wide, 48, scale)
    collect(e1_ref, wide, 64, scale)
    collect(e2_ref, wide, 96, scale)
    biases = wide[16, pl.ds(24, 8), :] * scale
    half = LANES // 2
    piece = jnp.where(lax.rem(lax.axis_index("rep"), 2) == 0, biases[:, :half], biases[:, half:])
    be_ref[...] = piece[0:1, :]
    bn_ref[...] = piece[1:2, :]


class Fetched:
    def __init__(self, ref, copy):
        self.ref, self.copy, self.shape = ref, copy, ref.shape
        self.started = self.ready = False

    def start(self):
        if not self.started:
            self.copy.start()
            self.started = True

    def wait(self):
        self.start()
        if not self.ready:
            self.copy.wait()
            self.ready = True
        return self.ref

    def __getitem__(self, at):
        return self.wait()[at]


class Written:
    def __init__(self, ref, out, copy):
        self.ref, self.out, self.copy, self.shape, self.sent = ref, out, copy, ref.shape, False

    def __setitem__(self, at, value):
        self.ref[at] = value

    def __getitem__(self, at):
        return self.ref[at]

    def flush(self):
        self.copy.start()
        self.sent = True

    def pieces(self, cuts, sems):
        self.sent = True
        self.copy = Many(
            [pltpu.make_async_copy(self.ref.at[c], self.out.at[c], sems.at[k]) for k, c in enumerate(cuts)]
        )
        return self.copy.copies


class Many:
    def __init__(self, copies):
        self.copies = copies

    def wait(self):
        for copy in self.copies:
            copy.wait()


HB = pl.BlockSpec(memory_space=pltpu.HBM)
SMALL, WIDE, RAW = 0, 1, 2


def call(kernel, name, kinds, outs, scratch, *args, raw_out=False, limit=VMEM_LIMIT, eager=99):
    fetched = [k for k, kind in enumerate(kinds) if kind != RAW]
    n_in, n_out = len(args), len(outs)

    def body(*refs):
        ins, results = refs[:n_in], refs[n_in : n_in + n_out]
        rest = list(refs[n_in + n_out :])
        in_sem, out_sem = rest.pop(0), rest.pop(0)
        given = list(ins)
        for at, k in enumerate(fetched):
            copy = pltpu.make_async_copy(ins[k], rest[at], in_sem.at[at])
            given[k] = Fetched(rest[at], copy)
            if k < eager:
                given[k].start()
        rest = rest[len(fetched) :]
        if raw_out:
            written = list(results)
        else:
            written = [
                Written(
                    rest[k], results[k], pltpu.make_async_copy(rest[k], results[k], out_sem.at[k])
                )
                for k in range(n_out)
            ]
            rest = rest[n_out:]
        kernel(*given, *written, *rest)
        for one in given:
            if isinstance(one, Fetched):
                one.wait()
        if not raw_out:
            for one in written:
                if not one.sent:
                    one.flush()
            for one in written:
                one.copy.wait()

    buffers = [
        (pltpu.SMEM if kinds[k] == SMALL else pltpu.VMEM)(args[k].shape, args[k].dtype)
        for k in fetched
    ]
    if not raw_out:
        buffers += [pltpu.VMEM(s, d) for s, d in outs]
    got = pl.pallas_call(
        body,
        name=name,
        out_shape=tuple(jax.ShapeDtypeStruct(s, d) for s, d in outs),
        in_specs=[HB] * n_in,
        out_specs=(HB,) * n_out,
        scratch_shapes=[
            pltpu.SemaphoreType.DMA((max(len(fetched), 1),)),
            pltpu.SemaphoreType.DMA((n_out,)),
            *buffers,
            *[s if not isinstance(s, tuple) else pltpu.VMEM(*s) for s in scratch],
        ],
        compiler_params=pltpu.CompilerParams(vmem_limit_bytes=limit),
    )(*args)
    return got[0] if n_out == 1 else got


def exchange(x, axis):
    return lax.all_to_all(x, axis, split_axis=0, concat_axis=0, tiled=True)


def on_device(
    nodes, cotangent, live, partner_first, partner_size, edge_src, edge_dst,
    w_edge1, b_edge, w_edge2, w_node1, b_node, w_node2,
):
    granules, block, width = nodes.shape[1:]
    rows = granules * block
    edges = edge_src.shape[1]
    hidden = w_edge1.shape[1]
    peers, reps = lax.axis_size("graph"), lax.axis_size("rep")
    blocks = nodes[0]
    flat = blocks.reshape(rows, width)
    cot = cotangent[0].reshape(rows, width)
    slots = peers * 2 * GMAX
    span = GMAX * block

    outgoing = call(
        pack_kernel, "pack", [SMALL, SMALL, WIDE], (((slots, block, width), BF16),),
        [((granules, block, width), BF16), pltpu.SemaphoreType.DMA((granules,))],
        live, partner_first, blocks, raw_out=True,
    )
    arrived = exchange(outgoing, "graph").reshape(2 * peers, span, width)
    flip, slope, near, lifted = call(
        edge_forward_kernel, "edge_forward", [WIDE] * 6 + [SMALL] + [WIDE] * 4,
        (
            ((2 * width + hidden, rows), BF16), ((edges, hidden), BF16),
            ((rows, hidden), F32), ((rows, hidden), F32),
        ),
        [
            ((rows, hidden), BF16), ((rows, hidden), BF16), ((edges, hidden), BF16),
            ((edges, LANES), jnp.int32), ((edges, LANES), jnp.int32),
        ],
        flat, w_edge1, b_edge.reshape(1, hidden), edge_dst, edge_src, w_edge2,
        live, cot, w_node1, b_node.reshape(1, hidden), w_node2,
    )
    probs, keys, grad_moved, active, hidden_grad, grad_t, grad_s, send = call(
        main_kernel, "main", [SMALL] * 3 + [WIDE] * 11,
        (
            ((rows, span), F32), ((granules * span, width), BF16), ((rows, width), BF16),
            ((rows, hidden), BF16), ((rows, hidden), BF16), ((rows, hidden), BF16),
            ((rows, hidden), BF16), ((reps * peers, 32, LANES), BF16),
        ),
        [
            ((rows, span), F32), ((rows, width), BF16), ((rows, width), BF16),
            ((rows, width), BF16), ((rows, hidden), BF16), ((edges, hidden), BF16),
            ((edges, LANES), jnp.int32), ((reps * peers, 32, LANES), F32),
            pltpu.SemaphoreType.DMA((2, rows // 1024)), pltpu.SemaphoreType.DMA((3,)),
        ],
        live, partner_first, partner_size, flat, arrived, near, w_node1, lifted,
        w_edge2, cot, flip, edge_dst, slope, edge_src, eager=5,
    )
    part = lax.psum_scatter(send, "rep", scatter_dimension=0, tiled=True)
    back_send, grad_scores = call(
        attend_back_kernel, "attend_back", [SMALL] + [WIDE] * 4,
        (((2 * peers, span, width), BF16), ((rows, span), BF16)),
        [((rows, span), F32)],
        partner_first, grad_moved, keys, probs, flat,
    )
    back_got = exchange(back_send.reshape(slots, block, width), "graph")
    part, back_got = lax.optimization_barrier((part, back_got))
    everything = exchange(
        call(
            share_sum_kernel, "share_sum", [WIDE], (((peers, 32, LANES), BF16),), [],
            exchange(part, "graph"), limit=SMALL_LIMIT,
        ),
        "graph",
    )
    scale = (peers * reps * rows) ** (-0.5)
    share = hidden // reps
    g_edge1, g_bedge, g_edge2, g_node1, g_bnode, g_node2 = call(
        functools.partial(unpack_kernel, scale), "unpack", [WIDE],
        (
            ((2 * width // reps, hidden), F32), ((1, share), F32), ((share, width), F32),
            ((3 * width // reps, hidden), F32), ((1, share), F32), ((share, width), F32),
        ),
        [((peers, 32, LANES), F32)],
        everything, limit=SMALL_LIMIT,
    )
    updated, d_nodes = call(
        finish_kernel, "finish", [SMALL] * 2 + [WIDE] * 13,
        (((rows, width), BF16), ((rows, width), BF16)),
        [((rows, width), F32)],
        live, partner_first, active, hidden_grad, w_node2, w_node1, flat, grad_t, grad_s, w_edge1,
        grad_scores, keys, grad_moved, cot, back_got,
    )
    return (
        updated.reshape(1, granules, block, width),
        d_nodes.reshape(1, granules, block, width),
        g_edge1, g_bedge.reshape(share), g_edge2, g_node1, g_bnode.reshape(share), g_node2,
    )


def solution(mesh):
    placed = (P("rep", "graph", None, None),) * 2 + (P("rep", "graph"),) * 5 + (P(),) * 6
    return jax.shard_map(
        on_device,
        mesh=mesh,
        in_specs=placed,
        out_specs=(
            P("rep", "graph", None, None),
            P("rep", "graph", None, None),
            P("rep", None),
            P("rep"),
            P("rep", None),
            P("rep", None),
            P("rep"),
            P("rep", None),
        ),
        check_vma=False,
    )
```
